256 devices in a mesh: role: 2 (over core), ctx: 4 (over y), req: 32 (over x, z).
Axes of the slice: x: 4, y: 4, z: 8, core: 2. Of those that a mesh axis runs over, the one named last changes fastest.
Arguments:
- cache: bfloat16 [64, 16384, 576], P(None, ('ctx', 'req'), 'role'), may hold values from -8 to 8
- lengths: int32 [64], replicated, may hold values from 2 to 16384
- request_decode_slot: int32 [64], replicated, may hold values from 0 to 63, as said below
- q_nope: bfloat16 [64, 4, 16384], P('req', None, ('role', 'ctx')), may hold values from -6 to 6
- q_rope: bfloat16 [64, 4, 8192], P('req', None, ('role', 'ctx')), may hold values from -8 to 8
- new_latent: bfloat16 [64, 4, 576], P('req'), may hold values from -4.1875 to 4.1875
- w_key: bfloat16 [128, 128, 512], P(('role', 'ctx')), may hold values from -0.5 to 0.5
- value_up_weight: bfloat16 [128, 512, 128], P(('role', 'ctx')), may hold values from -1 to 1
Outputs:
- attended: bfloat16 [64, 4, 16384], P('req', None, ('role', 'ctx'))
The draws below stay inside these ranges and needn't reach their ends.
Inputs may be any that keep to these rules, and one draw needn't show every extreme that they name: A permutation of the slots; request r is owned by req index request_decode_slot[r] // 2.
All inputs are finite; a program needn't handle non-finite values.
Results may differ from the reference program's by a relative error of at most 0.007.
Values may be sent and summed in bfloat16 or wider, within the bound.
No kernel may reach another device: no remote copies, remote signals or barrier semaphores. Data moves between devices by JAX's collectives and lax.ppermute only.
A program may use at most 128 MiB of HBM per device.

```python
import jax
import jax.numpy as jnp
from jax import lax

HEADS = 128
NOPE = 128
ROPE = 64
LATENT = 512
VDIM = 128
REQ_DEV = 2
BLOCK = 4096
STEPS = 4
REQS = 64
MAXLEN = 16384
N_CTX = 4
N_REQ = 32


def owner_table(key):
    return jax.random.permutation(jax.random.fold_in(key, 101), REQS).astype(jnp.int32)


def draw_request_decode_slot(key, part):
    return owner_table(key)


def draw_cache(key, part):
    base = jax.random.fold_in(key, 303)

    def one_request(index):
        first, second = jax.random.split(jax.random.fold_in(base, index))
        latent = jnp.clip(jax.random.normal(first, (MAXLEN, LATENT), jnp.float32) * 0.5, -3.0, 3.0)
        rotary = jnp.clip(jax.random.normal(second, (MAXLEN, ROPE), jnp.float32), -6.0, 6.0)
        return jnp.concatenate([latent, rotary], axis=1).astype(jnp.bfloat16)
    values = lax.map(one_request, jnp.arange(REQS, dtype=jnp.int32))
    return values


def draw_q_rope(key, part):
    values = jax.random.normal(jax.random.fold_in(key, 404), (REQS, STEPS, HEADS * ROPE), jnp.float32)
    values = jnp.clip(values, -6.0, 6.0)
    return values.astype(jnp.bfloat16)


def plant(drawn, stream_key, least, top_value):
    longest = drawn.shape.index(max(drawn.shape))
    spots = []
    for shift in (0, 1):
        where = [jax.random.randint(jax.random.fold_in(stream_key, axis), (), 0, length) for axis, length in enumerate(drawn.shape)]
        where[longest] = (where[longest] + shift) % drawn.shape[longest]
        spots.append(tuple(where))
    return drawn.at[spots[0]].set(least).at[spots[1]].set(top_value)


def shard_levels(key, dims, shards, least, largest):
    level = 1.0
    for position, shards_of in shards:
        draws = jax.random.uniform(jax.random.fold_in(jax.random.fold_in(key, 6), position), (shards_of,), jnp.float32, least / len(shards), largest / len(shards))
        level = level * jnp.repeat(jnp.exp(draws), dims[position] // shards_of).reshape((-1,) + (1,) * (len(dims) - 1 - position))
    return level


def noise(own_key, shape, deviation, reach, pieces=(), kind=jnp.bfloat16):
    gain = shard_levels(own_key, shape, pieces, -0.22, 0.18) if pieces else 1.0
    values = jax.random.normal(own_key, shape, jnp.float32) * deviation * gain
    return jnp.minimum(jnp.maximum(values, -reach), reach).astype(kind)


def setup_inputs(seed: int = 0) -> dict:
    key_of = jax.random.split(jax.random.key(seed), 9)
    return {
        "cache": draw_cache(jax.random.fold_in(key_of[8], 71), 0),
        "lengths": plant(jax.random.randint(key_of[1], (REQS,), 2, MAXLEN + 1), jax.random.fold_in(key_of[1], 1), 2, MAXLEN).astype(jnp.int32),
        "request_decode_slot": draw_request_decode_slot(jax.random.fold_in(key_of[8], 71), 0),
        "q_nope": noise(key_of[3], (REQS, STEPS, HEADS * NOPE), 1.0, 6.0, ((0, 32), (2, 8))),
        "q_rope": draw_q_rope(jax.random.fold_in(key_of[8], 71), 0),
        "new_latent": noise(key_of[5], (REQS, STEPS, LATENT + ROPE), 0.7, 4.1875, ((0, 32),)),
        "w_key": noise(key_of[6], (HEADS, NOPE, LATENT), NOPE ** -0.5, 0.5, ((0, 8),)),
        "value_up_weight": noise(key_of[7], (HEADS, LATENT, VDIM), (LATENT // 16) ** -0.5, 1.0, ((0, 8),)),
    }


def reference(cache, lengths, request_decode_slot, q_nope, q_rope, new_latent, w_key, value_up_weight):
    total_reqs = request_decode_slot.shape[0]
    inverse = jnp.zeros((total_reqs,), jnp.int32).at[request_decode_slot].set(jnp.arange(total_reqs, dtype=jnp.int32))
    softmax_scale = (NOPE + ROPE) ** -0.5
    key_weights = w_key.astype(jnp.float32)
    value_matrices = value_up_weight.astype(jnp.float32)
    step_ids = jnp.arange(STEPS, dtype=jnp.int32)
    causal = (step_ids[None, :] <= step_ids[:, None])[None, :, None, :]
    positions = jnp.arange(MAXLEN, dtype=jnp.int32)

    def one_owner(owner):
        first = (owner * REQ_DEV).astype(jnp.int32)
        requests = lax.dynamic_slice_in_dim(inverse, first, REQ_DEV)
        payload = cache[requests].astype(jnp.float32)
        visible = (positions[None, :] < lengths[requests][:, None])[:, None, None, :]
        queries = lax.dynamic_slice_in_dim(q_nope, first, REQ_DEV).astype(jnp.float32)
        queries = queries.reshape(REQ_DEV, STEPS, HEADS, NOPE)
        absorbed = jnp.einsum("gshd,hdk->gshk", queries, key_weights).astype(jnp.bfloat16)
        absorbed = lax.optimization_barrier(absorbed).astype(jnp.float32)
        rotary = lax.dynamic_slice_in_dim(q_rope, first, REQ_DEV).astype(jnp.float32)
        rotary = rotary.reshape(REQ_DEV, STEPS, HEADS, ROPE)
        query_rows = jnp.concatenate([absorbed, rotary], axis=3)
        fresh_rows = lax.dynamic_slice_in_dim(new_latent, first, REQ_DEV).astype(jnp.float32)
        scores = jnp.einsum("gshk,gpk->gshp", query_rows, payload) * softmax_scale
        fresh_scores = jnp.einsum("gshk,gtk->gsht", query_rows, fresh_rows) * softmax_scale
        highest = jnp.maximum(jnp.max(jnp.where(visible, scores, -1e30), axis=3),
                              jnp.max(jnp.where(causal, fresh_scores, -1e30), axis=3))
        weights = jnp.where(visible, jnp.exp(scores - highest[..., None]), 0.0)
        fresh_weights = jnp.where(causal, jnp.exp(fresh_scores - highest[..., None]), 0.0)
        normalizer = jnp.sum(weights, axis=3) + jnp.sum(fresh_weights, axis=3)
        rounded = lax.optimization_barrier(weights.astype(jnp.bfloat16)).astype(jnp.float32)
        rounded = rounded.reshape(REQ_DEV, STEPS, HEADS, N_CTX, BLOCK)
        fresh_rounded = lax.optimization_barrier(fresh_weights.astype(jnp.bfloat16)).astype(jnp.float32)
        latent_rows = payload[:, :, :LATENT].reshape(REQ_DEV, N_CTX, BLOCK, LATENT)
        partials = jnp.einsum("gshcp,gcpk->gshck", rounded, latent_rows)
        fresh_part = jnp.einsum("gsht,gtk->gshk", fresh_rounded, fresh_rows[:, :, :LATENT])
        partials = partials.at[:, :, :, 0].add(fresh_part)
        partials = lax.optimization_barrier(partials.astype(jnp.bfloat16)).astype(jnp.float32)
        numerators = jnp.sum(partials, axis=3)
        combined_result = (numerators / normalizer[..., None]).astype(jnp.bfloat16)
        combined_result = lax.optimization_barrier(combined_result).astype(jnp.float32)
        output_rows = jnp.einsum("jnay,ayp->jnap", combined_result, value_matrices).astype(jnp.bfloat16)
        return output_rows.reshape(REQ_DEV, STEPS, HEADS * VDIM)

    stacked = lax.map(one_owner, jnp.arange(N_REQ, dtype=jnp.int32))
    return stacked.reshape(total_reqs, STEPS, HEADS * VDIM)
```

```python
import functools

import jax
import jax.numpy as jnp
from jax import lax
from jax.experimental import pallas as pl
from jax.experimental.pallas import tpu as pltpu
from jax.sharding import PartitionSpec as P

NX, NZ = 4, 8
NC = 4
LANES = 128
NEG = -1e30


def z_to(z, c):
    return (z + (0, 1, -1, 2 if z % 2 == 0 else -2)[c]) % NZ


def move_z(a, c):
    if c == 0:
        return a
    return lax.ppermute(a, "req", [(x * NZ + z, x * NZ + z_to(z, c)) for x in range(NX) for z in range(NZ)])


def move_x(a, dx):
    if dx == 0:
        return a
    return lax.ppermute(a, "req", [(x * NZ + z, (x + dx) % NX * NZ + z) for x in range(NX) for z in range(NZ)])


def move_far(a):
    return lax.ppermute(a, "req", [(x * NZ + z, x * NZ + (z + 4) % NZ) for x in range(NX) for z in range(NZ)])


def swap_role(a):
    return lax.ppermute(a, "role", [(0, 1), (1, 0)])


def lookup(slots, values, want):
    return jnp.sum(jnp.where(slots == want[..., None], values, 0), axis=-1)


def pick_kernel(idx_ref, k_ref, *rest):
    outs, sems = rest[:-1], rest[-1]
    copies = []
    for o, out in enumerate(outs):
        for i in range(4):
            n = o * 4 + i
            copies.append(pltpu.make_async_copy(k_ref.at[idx_ref[n]], out.at[i], sems.at[n]))
    for c in copies:
        c.start()
    for c in copies:
        c.wait()


def pick(k, idx):
    block = k.shape[1:]
    return pl.pallas_call(
        pick_kernel,
        grid_spec=pltpu.PrefetchScalarGridSpec(
            num_scalar_prefetch=1,
            grid=(),
            in_specs=[pl.BlockSpec(memory_space=pl.ANY)],
            out_specs=[pl.BlockSpec(memory_space=pl.ANY)] * 8,
            scratch_shapes=[pltpu.SemaphoreType.DMA((32,))],
        ),
        out_shape=[jax.ShapeDtypeStruct((4, *block), k.dtype)] * 8,
        cost_estimate=pl.CostEstimate(flops=0, bytes_accessed=2 * 32 * block[0] * block[1] * 2, transcendentals=0),
    )(idx, k)


def attend_kernel(fresh, scale, scal_ref, q_ref, *rest):
    mine, recv = rest[:4], rest[4:8]
    rest = rest[8:]
    if fresh:
        new_ref, rest = rest[0], rest[1:]
    o_ref, kt, s_ref = rest
    half = mine[0].shape[1]
    latent = o_ref.shape[1] - LANES
    rows = q_ref.shape[0]
    role = scal_ref[16]
    at_mine = pl.ds(pl.multiple_of(role * half, 32), half)
    at_recv = pl.ds(pl.multiple_of((1 - role) * half, 32), half)
    chunk = 4 * LANES
    lane = lax.broadcasted_iota(jnp.int32, (1, LANES), 1)
    high = jnp.full((rows, LANES), NEG, jnp.float32)
    for j in range(4):
        for c in range(4):
            cols = slice(j * chunk + c * LANES, j * chunk + (c + 1) * LANES)
            kt[at_mine, cols] = mine[c][j]
            kt[at_recv, cols] = recv[j][c]
        s = jnp.dot(q_ref[...], kt[:, j * chunk:(j + 1) * chunk], preferred_element_type=jnp.float32)
        for c in range(4):
            t = s[:, c * LANES:(c + 1) * LANES] * scale
            t = jnp.where(lane < scal_ref[j * 4 + c], t, NEG)
            s_ref[:, j * chunk + c * LANES:j * chunk + (c + 1) * LANES] = t
            high = jnp.maximum(high, t)
    if fresh:
        t = jnp.dot(q_ref[...], new_ref[...], preferred_element_type=jnp.float32) * scale
        step = (lax.broadcasted_iota(jnp.int32, (rows, LANES), 0) // 16) % 4
        u = lax.broadcasted_iota(jnp.int32, (rows, LANES), 1)
        f = jnp.where((u <= step) & (scal_ref[17] == 0), t, NEG)
        high = jnp.maximum(high, f)
    m = jnp.maximum(jnp.max(high, axis=1, keepdims=True), -1e29)
    total = jnp.zeros((rows, LANES), jnp.float32)
    acc = jnp.zeros((rows, latent), jnp.float32)
    nt = (((1,), (1,)), ((), ()))
    for j in range(4):
        w = jnp.exp(s_ref[:, j * chunk:(j + 1) * chunk] - m)
        for c in range(4):
            total = total + w[:, c * LANES:(c + 1) * LANES]
        acc = acc + lax.dot_general(w.astype(jnp.bfloat16), kt[:latent, j * chunk:(j + 1) * chunk], nt,
                                    preferred_element_type=jnp.float32)
    if fresh:
        w = jnp.exp(f - m)
        total = total + w
        acc = acc + lax.dot_general(w.astype(jnp.bfloat16), new_ref[:latent, :], nt, preferred_element_type=jnp.float32)
    norm = jnp.sum(total, axis=1, keepdims=True)
    some = norm > 0.0
    safe = jnp.where(some, norm, 1.0)
    o_ref[:, :latent] = (acc / safe).astype(jnp.bfloat16)
    lse = jnp.where(some, m + jnp.log(safe), NEG)
    o_ref[:, latent:] = pack_columns(lse, lax.broadcasted_iota(jnp.int32, (rows, LANES), 1))


def pack_columns(lse, lane):
    a = lse.astype(jnp.bfloat16).astype(jnp.float32)
    b = (lse - a).astype(jnp.bfloat16).astype(jnp.float32)
    c = (lse - a) - b
    return jnp.where(lane == 0, a, jnp.where(lane == 1, b, jnp.where(lane == 2, c, 0.0))).astype(jnp.bfloat16)


def attend(scal, q, mine, recv, new, latent, scale):
    rows, width = q.shape
    fresh = new is not None
    vm = pl.BlockSpec(memory_space=pltpu.VMEM)
    args = [q, *mine, *recv] + ([new] if fresh else [])
    positions = 16 * LANES
    return pl.pallas_call(
        functools.partial(attend_kernel, fresh, scale),
        in_specs=[pl.BlockSpec(memory_space=pltpu.SMEM)] + [vm] * len(args),
        out_specs=vm,
        out_shape=jax.ShapeDtypeStruct((rows, latent + LANES), jnp.bfloat16),
        scratch_shapes=[pltpu.VMEM((width, positions), jnp.bfloat16), pltpu.VMEM((rows, positions), jnp.float32)],
        compiler_params=pltpu.CompilerParams(vmem_limit_bytes=40 * 1024 * 1024),
        cost_estimate=pl.CostEstimate(flops=2 * rows * positions * (width + latent),
                                      bytes_accessed=positions * width * 2 + rows * (width + latent) * 2,
                                      transcendentals=rows * positions),
    )(scal, *args)


def merge(parts, latent, axis):
    lse = jnp.sum(parts[..., latent:latent + 3].astype(jnp.float32), axis=-1, keepdims=True)
    top = jnp.max(lse, axis=axis, keepdims=True)
    w = jnp.exp(lse - top)
    norm = jnp.sum(w, axis=axis)
    rows = jnp.sum(parts[..., :latent].astype(jnp.float32) * w, axis=axis) / norm
    return rows, jnp.squeeze(top, axis) + jnp.log(norm)


def two_way(picked):
    by_x, away = picked[:4], picked[4:]
    order = (1, 2, 3, 0)
    got_role = {c: swap_role(away[c]) for c in order}
    got_x = [move_x(by_x[dx], dx) for dx in range(4)]
    got_z = [move_z(got_role[c], c) for c in range(4)]
    mine = [move_z(jnp.stack([got_x[dx][c] for dx in range(4)]), c) for c in range(4)]
    recv = [move_x(jnp.stack([got_z[c][dx] for c in range(4)]), dx) for dx in range(4)]
    return mine, recv


def shards(cache, lengths, request_decode_slot, q_nope, q_rope, new_latent, w_key, value_up_weight):
    heads_dev, nope_dim, latent = w_key.shape
    req_dev, steps = q_nope.shape[:2]
    rope_dim = q_rope.shape[2] // heads_dev
    scale = (nope_dim + rope_dim) ** -0.5
    role, ctx, req = lax.axis_index("role"), lax.axis_index("ctx"), lax.axis_index("req")
    x, z = req // NZ, req % NZ
    total = request_decode_slot.shape[0]
    ids = jnp.arange(total, dtype=jnp.int32)
    dx = jnp.arange(NX, dtype=jnp.int32)[:, None]
    cls = jnp.arange(NC, dtype=jnp.int32)
    move = jnp.where(cls == 1, 1, jnp.where(cls == 2, -1, jnp.where(cls == 3, jnp.where(z % 2 == 0, 2, -2), 0)))[None, :]
    blocks = jnp.swapaxes(cache, 1, 2)

    picked = []
    for far in (4, 0):
        owner = (x + dx) % NX * NZ + (z + move + far + NZ) % NZ
        want = jnp.concatenate([(2 * owner + role).reshape(-1), (2 * owner + 1 - role).T.reshape(-1)])
        picked.append(pick(blocks, lookup(request_decode_slot, ids, want)))
    source = (x - dx + NX) % NX * NZ + (z - move + NZ) % NZ
    base = ctx * (NX * NZ * LANES) + source * LANES

    def scalars(far):
        want = 2 * (x * NZ + (z + far) % NZ) + role
        length = lookup(request_decode_slot, lengths, want)
        return jnp.concatenate([(length - base).reshape(-1), role[None], ctx[None]]).astype(jnp.int32)

    queries = q_nope.reshape(req_dev, steps, heads_dev, nope_dim)
    absorbed = jnp.einsum("bshd,hdk->bshk", queries, w_key, preferred_element_type=jnp.float32).astype(jnp.bfloat16)
    own = jnp.concatenate([absorbed, q_rope.reshape(req_dev, steps, heads_dev, rope_dim)], axis=3)
    both = jnp.stack([own, move_far(own)], axis=1)
    keep = jnp.where(role == 0, both[0], both[1])
    got = swap_role(jnp.where(role == 0, both[1], both[0]))
    pair = jnp.stack([jnp.where(role == 0, keep, got), jnp.where(role == 0, got, keep)], axis=1)
    every = lax.all_gather(pair, "ctx", axis=2, tiled=False)
    every = every.reshape(2, -1, latent + rope_dim)

    mine_f, recv_f = two_way(picked[0])
    near, mine_f, recv_f = lax.optimization_barrier((picked[1], mine_f, recv_f))
    part_f = attend(scalars(4), every[1], mine_f, recv_f, None, latent, scale)
    mine_n, recv_n = two_way(near)
    heads = 2 * lax.axis_size("ctx")
    part_f = lax.all_to_all(part_f.reshape(heads, -1, latent + LANES), ("role", "ctx"), 0, 0, tiled=True)
    rows_f, lse_f = merge(part_f.reshape(2, -1, *part_f.shape[1:]), latent, 1)
    packed = jnp.concatenate(
        [rows_f.astype(jnp.bfloat16), pack_columns(lse_f, lax.broadcasted_iota(jnp.int32, (*lse_f.shape[:2], LANES), 2))], axis=-1)
    packed = move_far(packed)

    new = jnp.where(role == 0, new_latent[0], new_latent[1])
    new = jnp.pad(new.T, ((0, 0), (0, LANES - steps)))
    part_n = attend(scalars(0), every[0], mine_n, recv_n, new, latent, scale)
    part_n = lax.all_to_all(part_n.reshape(heads, -1, latent + LANES), ("role", "ctx"), 0, 0, tiled=True)
    parts = jnp.concatenate([part_n.reshape(2, -1, *part_n.shape[1:]), packed[:, None]], axis=1)
    merged, _ = merge(parts, latent, 1)
    merged = merged.astype(jnp.bfloat16).reshape(req_dev, steps, heads_dev, latent)
    out = jnp.einsum("bshk,hkv->bshv", merged, value_up_weight, preferred_element_type=jnp.float32).astype(jnp.bfloat16)
    return out.reshape(req_dev, steps, -1)


def solution(mesh):
    placed = (
        P(None, ("ctx", "req"), "role"),
        P(),
        P(),
        P("req", None, ("role", "ctx")),
        P("req", None, ("role", "ctx")),
        P("req", None, None),
        P(("role", "ctx"), None, None),
        P(("role", "ctx"), None, None),
    )
    return jax.shard_map(
        shards,
        mesh=mesh,
        in_specs=placed,
        out_specs=P("req", None, ("role", "ctx")),
        check_vma=False,
    )
```

```python
import functools

import jax
import jax.numpy as jnp
from jax import lax
from jax.experimental import pallas as pl
from jax.experimental.pallas import tpu as pltpu
from jax.sharding import PartitionSpec as P

NX, NZ = 4, 8
NC = 4
LANES = 128
NEG = -1e30


def z_to(z, c):
    return (z + (0, 1, -1, 2 if z % 2 == 0 else -2)[c]) % NZ


def move_z(a, c):
    if c == 0:
        return a
    return lax.ppermute(a, "req", [(x * NZ + z, x * NZ + z_to(z, c)) for x in range(NX) for z in range(NZ)])


def move_x(a, dx):
    if dx == 0:
        return a
    return lax.ppermute(a, "req", [(x * NZ + z, (x + dx) % NX * NZ + z) for x in range(NX) for z in range(NZ)])


def move_far(a):
    return lax.ppermute(a, "req", [(x * NZ + z, x * NZ + (z + 4) % NZ) for x in range(NX) for z in range(NZ)])


def swap_role(a):
    return lax.ppermute(a, "role", [(0, 1), (1, 0)])


def lookup(slots, values, want):
    return jnp.sum(jnp.where(slots == want[..., None], values, 0), axis=-1)


def attend_kernel(fresh, scale, scal_ref, q_ref, *rest):
    mine, recv = rest[:4], rest[4:8]
    rest = rest[8:]
    if fresh:
        new_ref, rest = rest[0], rest[1:]
    o_ref, kt, s_ref = rest
    half = mine[0].shape[1]
    latent = o_ref.shape[1] - LANES
    rows = q_ref.shape[0]
    role = scal_ref[16]
    at_mine = pl.ds(pl.multiple_of(role * half, 32), half)
    at_recv = pl.ds(pl.multiple_of((1 - role) * half, 32), half)
    chunk = 4 * LANES
    lane = lax.broadcasted_iota(jnp.int32, (1, LANES), 1)
    high = jnp.full((rows, LANES), NEG, jnp.float32)
    for j in range(4):
        for c in range(4):
            cols = slice(j * chunk + c * LANES, j * chunk + (c + 1) * LANES)
            kt[at_mine, cols] = mine[c][j]
            kt[at_recv, cols] = recv[j][c]
        s = jnp.dot(q_ref[...], kt[:, j * chunk:(j + 1) * chunk], preferred_element_type=jnp.float32)
        for c in range(4):
            t = s[:, c * LANES:(c + 1) * LANES] * scale
            t = jnp.where(lane < scal_ref[j * 4 + c], t, NEG)
            s_ref[:, j * chunk + c * LANES:j * chunk + (c + 1) * LANES] = t
            high = jnp.maximum(high, t)
    if fresh:
        t = jnp.dot(q_ref[...], new_ref[...], preferred_element_type=jnp.float32) * scale
        step = (lax.broadcasted_iota(jnp.int32, (rows, LANES), 0) // 16) % 4
        u = lax.broadcasted_iota(jnp.int32, (rows, LANES), 1)
        f = jnp.where((u <= step) & (scal_ref[17] == 0), t, NEG)
        high = jnp.maximum(high, f)
    m = jnp.maximum(jnp.max(high, axis=1, keepdims=True), -1e29)
    total = jnp.zeros((rows, LANES), jnp.float32)
    acc = jnp.zeros((rows, latent), jnp.float32)
    nt = (((1,), (1,)), ((), ()))
    for j in range(4):
        w = jnp.exp(s_ref[:, j * chunk:(j + 1) * chunk] - m)
        for c in range(4):
            total = total + w[:, c * LANES:(c + 1) * LANES]
        acc = acc + lax.dot_general(w.astype(jnp.bfloat16), kt[:latent, j * chunk:(j + 1) * chunk], nt,
                                    preferred_element_type=jnp.float32)
    if fresh:
        w = jnp.exp(f - m)
        total = total + w
        acc = acc + lax.dot_general(w.astype(jnp.bfloat16), new_ref[:latent, :], nt, preferred_element_type=jnp.float32)
    norm = jnp.sum(total, axis=1, keepdims=True)
    some = norm > 0.0
    safe = jnp.where(some, norm, 1.0)
    o_ref[:, :latent] = (acc / safe).astype(jnp.bfloat16)
    lse = jnp.where(some, m + jnp.log(safe), NEG)
    o_ref[:, latent:] = pack_columns(lse, lax.broadcasted_iota(jnp.int32, (rows, LANES), 1))


def pack_columns(lse, lane):
    a = lse.astype(jnp.bfloat16).astype(jnp.float32)
    b = (lse - a).astype(jnp.bfloat16).astype(jnp.float32)
    c = (lse - a) - b
    return jnp.where(lane == 0, a, jnp.where(lane == 1, b, jnp.where(lane == 2, c, 0.0))).astype(jnp.bfloat16)


def attend(scal, q, mine, recv, new, latent, scale):
    rows, width = q.shape
    fresh = new is not None
    vm = pl.BlockSpec(memory_space=pltpu.VMEM)
    args = [q, *mine, *recv] + ([new] if fresh else [])
    positions = 16 * LANES
    return pl.pallas_call(
        functools.partial(attend_kernel, fresh, scale),
        in_specs=[pl.BlockSpec(memory_space=pltpu.SMEM)] + [vm] * len(args),
        out_specs=vm,
        out_shape=jax.ShapeDtypeStruct((rows, latent + LANES), jnp.bfloat16),
        scratch_shapes=[pltpu.VMEM((width, positions), jnp.bfloat16), pltpu.VMEM((rows, positions), jnp.float32)],
        compiler_params=pltpu.CompilerParams(vmem_limit_bytes=40 * 1024 * 1024),
        cost_estimate=pl.CostEstimate(flops=2 * rows * positions * (width + latent),
                                      bytes_accessed=positions * width * 2 + rows * (width + latent) * 2,
                                      transcendentals=rows * positions),
    )(scal, *args)


def merge(parts, latent, axis):
    lse = jnp.sum(parts[..., latent:latent + 3].astype(jnp.float32), axis=-1, keepdims=True)
    top = jnp.max(lse, axis=axis, keepdims=True)
    w = jnp.exp(lse - top)
    norm = jnp.sum(w, axis=axis)
    rows = jnp.sum(parts[..., :latent].astype(jnp.float32) * w, axis=axis) / norm
    return rows, jnp.squeeze(top, axis) + jnp.log(norm)


def after(v, dep):
    return lax.optimization_barrier((v, dep))[0]


def exchange(by_x, away):
    got_x, got_z = [None] * 4, [None] * 4
    for i in (1, 2, 3, 0):
        got_z[i] = swap_role(away[i])
    for i in (1, 2, 3, 0):
        got_x[i] = move_x(by_x[i], i)
        got_z[i] = move_z(got_z[i], i)
    sides = []
    mine, recv = [None] * 4, [None] * 4
    for g in range(2):
        mine = [move_z(after(jnp.stack([got_x[d][g, c] for d in range(4)]), mine[c]), c) for c in range(4)]
        recv = [move_x(after(jnp.stack([got_z[c][g, d] for c in range(4)]), recv[d]), d) for d in range(4)]
        sides.append((mine, recv))
    return sides


def shards(cache, lengths, request_decode_slot, q_nope, q_rope, new_latent, w_key, value_up_weight):
    heads_dev, nope_dim, latent = w_key.shape
    req_dev, steps = q_nope.shape[:2]
    rope_dim = q_rope.shape[2] // heads_dev
    scale = (nope_dim + rope_dim) ** -0.5
    role, ctx, req = lax.axis_index("role"), lax.axis_index("ctx"), lax.axis_index("req")
    x, z = req // NZ, req % NZ
    total = request_decode_slot.shape[0]
    ids = jnp.arange(total, dtype=jnp.int32)
    dx = jnp.arange(NX, dtype=jnp.int32)[:, None]
    cls = jnp.arange(NC, dtype=jnp.int32)
    move = jnp.where(cls == 1, 1, jnp.where(cls == 2, -1, jnp.where(cls == 3, jnp.where(z % 2 == 0, 2, -2), 0)))[None, :]
    blocks = jnp.swapaxes(cache, 1, 2)

    far = jnp.array([4, 0], jnp.int32)[:, None, None]
    owner = (x + dx) % NX * NZ + (z + move + far + NZ) % NZ
    take_x = lookup(request_decode_slot, ids, 2 * owner + role)
    take_z = lookup(request_decode_slot, ids, 2 * owner + 1 - role)
    by_x = [blocks[take_x[:, d]] for d in range(NX)]
    away = [blocks[take_z[:, :, c]] for c in range(NC)]
    source = (x - dx + NX) % NX * NZ + (z - move + NZ) % NZ
    base = ctx * (NX * NZ * LANES) + source * LANES

    def scalars(far):
        want = 2 * (x * NZ + (z + far) % NZ) + role
        length = lookup(request_decode_slot, lengths, want)
        return jnp.concatenate([(length - base).reshape(-1), role[None], ctx[None]]).astype(jnp.int32)

    queries = q_nope.reshape(req_dev, steps, heads_dev, nope_dim)
    absorbed = jnp.einsum("bshd,hdk->bshk", queries, w_key, preferred_element_type=jnp.float32).astype(jnp.bfloat16)
    own = jnp.concatenate([absorbed, q_rope.reshape(req_dev, steps, heads_dev, rope_dim)], axis=3)
    both = jnp.stack([own, move_far(own)], axis=1)
    keep = jnp.where(role == 0, both[0], both[1])
    got = swap_role(jnp.where(role == 0, both[1], both[0]))
    pair = jnp.stack([jnp.where(role == 0, keep, got), jnp.where(role == 0, got, keep)], axis=1)
    every = lax.all_gather(pair, "ctx", axis=2, tiled=False)
    every = every.reshape(2, -1, latent + rope_dim)

    (mine_f, recv_f), (mine_n, recv_n) = exchange(by_x, away)
    part_f = attend(scalars(4), every[1], mine_f, recv_f, None, latent, scale)
    heads = 2 * lax.axis_size("ctx")
    part_f = lax.all_to_all(part_f.reshape(heads, -1, latent + LANES), ("role", "ctx"), 0, 0, tiled=True)
    rows_f, lse_f = merge(part_f.reshape(2, -1, *part_f.shape[1:]), latent, 1)
    packed = jnp.concatenate(
        [rows_f.astype(jnp.bfloat16), pack_columns(lse_f, lax.broadcasted_iota(jnp.int32, (*lse_f.shape[:2], LANES), 2))], axis=-1)
    packed = move_far(packed)

    new = jnp.where(role == 0, new_latent[0], new_latent[1])
    new = jnp.pad(new.T, ((0, 0), (0, LANES - steps)))
    part_n = attend(scalars(0), every[0], mine_n, recv_n, new, latent, scale)
    part_n = lax.all_to_all(part_n.reshape(heads, -1, latent + LANES), ("role", "ctx"), 0, 0, tiled=True)
    parts = jnp.concatenate([part_n.reshape(2, -1, *part_n.shape[1:]), packed[:, None]], axis=1)
    merged, _ = merge(parts, latent, 1)
    merged = merged.astype(jnp.bfloat16).reshape(req_dev, steps, heads_dev, latent)
    out = jnp.einsum("bshk,hkv->bshv", merged, value_up_weight, preferred_element_type=jnp.float32).astype(jnp.bfloat16)
    return out.reshape(req_dev, steps, -1)


def solution(mesh):
    placed = (
        P(None, ("ctx", "req"), "role"),
        P(),
        P(),
        P("req", None, ("role", "ctx")),
        P("req", None, ("role", "ctx")),
        P("req", None, None),
        P(("role", "ctx"), None, None),
        P(("role", "ctx"), None, None),
    )
    return jax.shard_map(
        shards,
        mesh=mesh,
        in_specs=placed,
        out_specs=P("req", None, ("role", "ctx")),
        check_vma=False,
    )
```

```python
import functools

import jax
import jax.numpy as jnp
from jax import lax
from jax.experimental import pallas as pl
from jax.experimental.pallas import tpu as pltpu
from jax.sharding import PartitionSpec as P

NX, NZ = 4, 8
NC = 4
LANES = 128
NEG = -1e30


def z_to(z, c):
    return (z + (0, 1, -1, 2 if z % 2 == 0 else -2)[c]) % NZ


def move_z(a, c, flip=0):
    if c == 0 and not flip:
        return a
    n = NX * NZ
    pairs = [(r * n + x * NZ + z, (r ^ flip) * n + x * NZ + z_to(z, c)) for r in range(2) for x in range(NX) for z in range(NZ)]
    return lax.ppermute(a, ("role", "req"), pairs)


def move_x(a, dx):
    if dx == 0:
        return a
    return lax.ppermute(a, "req", [(x * NZ + z, (x + dx) % NX * NZ + z) for x in range(NX) for z in range(NZ)])


def move_far(a):
    return lax.ppermute(a, "req", [(x * NZ + z, x * NZ + (z + 4) % NZ) for x in range(NX) for z in range(NZ)])


def swap_role(a):
    return lax.ppermute(a, "role", [(0, 1), (1, 0)])


def lookup(slots, values, want):
    return jnp.sum(jnp.where(slots == want[..., None], values, 0), axis=-1)


def pick_kernel(idx_ref, k_ref, *outs):
    for o, out in enumerate(outs):
        for g in range(2):
            for i in range(4):
                out[g, i] = k_ref[idx_ref[o * 8 + g * 4 + i]]


def pick(k, idx):
    vm = pl.BlockSpec(memory_space=pltpu.VMEM)
    block = k.shape[1:]
    return pl.pallas_call(
        pick_kernel,
        in_specs=[pl.BlockSpec(memory_space=pltpu.SMEM), vm],
        out_specs=[vm] * 8,
        out_shape=[jax.ShapeDtypeStruct((2, 4, *block), k.dtype)] * 8,
        compiler_params=pltpu.CompilerParams(vmem_limit_bytes=32 * 1024 * 1024),
        cost_estimate=pl.CostEstimate(flops=0, bytes_accessed=2 * 64 * block[0] * block[1] * 2, transcendentals=0),
    )(idx, k)


def regroup_kernel(*refs):
    for g in range(2):
        for i in range(4):
            for j in range(4):
                refs[4 + g * 4 + i][j] = refs[j][g, i]


def regroup(parts):
    vm = pl.BlockSpec(memory_space=pltpu.VMEM)
    shape = parts[0].shape[1:]
    size = shape[0] * shape[1] * shape[2]
    return pl.pallas_call(
        regroup_kernel,
        in_specs=[vm] * 4,
        out_specs=[vm] * 8,
        out_shape=[jax.ShapeDtypeStruct(shape, parts[0].dtype)] * 8,
        compiler_params=pltpu.CompilerParams(vmem_limit_bytes=32 * 1024 * 1024),
        cost_estimate=pl.CostEstimate(flops=0, bytes_accessed=2 * 8 * size * 2, transcendentals=0),
    )(*parts)


def attend_kernel(fresh, scale, scal_ref, q_ref, *rest):
    mine, recv = rest[:4], rest[4:8]
    rest = rest[8:]
    if fresh:
        new_ref, rest = rest[0], rest[1:]
    o_ref, kt, s_ref = rest
    half = mine[0].shape[1]
    latent = o_ref.shape[1] - LANES
    rows = q_ref.shape[0]
    role = scal_ref[16]
    at_mine = pl.ds(pl.multiple_of(role * half, 32), half)
    at_recv = pl.ds(pl.multiple_of((1 - role) * half, 32), half)
    chunk = 4 * LANES
    lane = lax.broadcasted_iota(jnp.int32, (1, LANES), 1)
    high = jnp.full((rows, LANES), NEG, jnp.float32)
    for j in range(4):
        for c in range(4):
            cols = slice(j * chunk + c * LANES, j * chunk + (c + 1) * LANES)
            kt[at_mine, cols] = mine[c][j]
            kt[at_recv, cols] = recv[j][c]
        s = jnp.dot(q_ref[...], kt[:, j * chunk:(j + 1) * chunk], preferred_element_type=jnp.float32)
        for c in range(4):
            t = s[:, c * LANES:(c + 1) * LANES] * scale
            t = jnp.where(lane < scal_ref[j * 4 + c], t, NEG)
            s_ref[:, j * chunk + c * LANES:j * chunk + (c + 1) * LANES] = t
            high = jnp.maximum(high, t)
    if fresh:
        t = jnp.dot(q_ref[...], new_ref[...], preferred_element_type=jnp.float32) * scale
        step = (lax.broadcasted_iota(jnp.int32, (rows, LANES), 0) // 16) % 4
        u = lax.broadcasted_iota(jnp.int32, (rows, LANES), 1)
        f = jnp.where((u <= step) & (scal_ref[17] == 0), t, NEG)
        high = jnp.maximum(high, f)
    m = jnp.maximum(jnp.max(high, axis=1, keepdims=True), -1e29)
    total = jnp.zeros((rows, LANES), jnp.float32)
    acc = jnp.zeros((rows, latent), jnp.float32)
    nt = (((1,), (1,)), ((), ()))
    for j in range(4):
        w = jnp.exp(s_ref[:, j * chunk:(j + 1) * chunk] - m)
        for c in range(4):
            total = total + w[:, c * LANES:(c + 1) * LANES]
        acc = acc + lax.dot_general(w.astype(jnp.bfloat16), kt[:latent, j * chunk:(j + 1) * chunk], nt,
                                    preferred_element_type=jnp.float32)
    if fresh:
        w = jnp.exp(f - m)
        total = total + w
        acc = acc + lax.dot_general(w.astype(jnp.bfloat16), new_ref[:latent, :], nt, preferred_element_type=jnp.float32)
    norm = jnp.sum(total, axis=1, keepdims=True)
    some = norm > 0.0
    safe = jnp.where(some, norm, 1.0)
    o_ref[:, :latent] = (acc / safe).astype(jnp.bfloat16)
    lse = jnp.where(some, m + jnp.log(safe), NEG)
    o_ref[:, latent:] = pack_columns(lse, lax.broadcasted_iota(jnp.int32, (rows, LANES), 1))


def pack_columns(lse, lane):
    a = lse.astype(jnp.bfloat16).astype(jnp.float32)
    b = (lse - a).astype(jnp.bfloat16).astype(jnp.float32)
    c = (lse - a) - b
    return jnp.where(lane == 0, a, jnp.where(lane == 1, b, jnp.where(lane == 2, c, 0.0))).astype(jnp.bfloat16)


def attend(scal, q, mine, recv, new, latent, scale):
    rows, width = q.shape
    fresh = new is not None
    vm = pl.BlockSpec(memory_space=pltpu.VMEM)
    args = [q, *mine, *recv] + ([new] if fresh else [])
    positions = 16 * LANES
    return pl.pallas_call(
        functools.partial(attend_kernel, fresh, scale),
        in_specs=[pl.BlockSpec(memory_space=pltpu.SMEM)] + [vm] * len(args),
        out_specs=vm,
        out_shape=jax.ShapeDtypeStruct((rows, latent + LANES), jnp.bfloat16),
        scratch_shapes=[pltpu.VMEM((width, positions), jnp.bfloat16), pltpu.VMEM((rows, positions), jnp.float32)],
        compiler_params=pltpu.CompilerParams(vmem_limit_bytes=40 * 1024 * 1024),
        cost_estimate=pl.CostEstimate(flops=2 * rows * positions * (width + latent),
                                      bytes_accessed=positions * width * 2 + rows * (width + latent) * 2,
                                      transcendentals=rows * positions),
    )(scal, *args)


def merge(parts, latent, axis):
    lse = jnp.sum(parts[..., latent:latent + 3].astype(jnp.float32), axis=-1, keepdims=True)
    top = jnp.max(lse, axis=axis, keepdims=True)
    w = jnp.exp(lse - top)
    norm = jnp.sum(w, axis=axis)
    rows = jnp.sum(parts[..., :latent].astype(jnp.float32) * w, axis=axis) / norm
    return rows, jnp.squeeze(top, axis) + jnp.log(norm)


def after(v, dep):
    return lax.optimization_barrier((v, dep))[0]


def second(parts, move):
    parts = regroup(parts)
    far = [move(parts[i], i) for i in range(4)]
    near = [move(after(parts[4 + i], far[i]), i) for i in range(4)]
    return far, near


def shards(cache, lengths, request_decode_slot, q_nope, q_rope, new_latent, w_key, value_up_weight):
    heads_dev, nope_dim, latent = w_key.shape
    req_dev, steps = q_nope.shape[:2]
    rope_dim = q_rope.shape[2] // heads_dev
    scale = (nope_dim + rope_dim) ** -0.5
    role, ctx, req = lax.axis_index("role"), lax.axis_index("ctx"), lax.axis_index("req")
    x, z = req // NZ, req % NZ
    total = request_decode_slot.shape[0]
    ids = jnp.arange(total, dtype=jnp.int32)
    dx = jnp.arange(NX, dtype=jnp.int32)[:, None]
    cls = jnp.arange(NC, dtype=jnp.int32)
    move = jnp.where(cls == 1, 1, jnp.where(cls == 2, -1, jnp.where(cls == 3, jnp.where(z % 2 == 0, 2, -2), 0)))[None, :]
    blocks = jnp.swapaxes(cache, 1, 2)

    far = jnp.array([4, 0], jnp.int32)[:, None, None]
    owner = (x + dx) % NX * NZ + (z + move + far + NZ) % NZ
    take_x = lookup(request_decode_slot, ids, 2 * owner + role)
    take_z = lookup(request_decode_slot, ids, 2 * owner + 1 - role)
    index = jnp.concatenate([jnp.moveaxis(take_z, 2, 0).reshape(-1), jnp.moveaxis(take_x, 1, 0).reshape(-1)])
    picked = pick(blocks, index)
    got_z = [None, move_z(picked[1], 1, 1), move_z(picked[2], 2, 1), None]
    got_x = [picked[4], move_x(picked[5], 1), None, move_x(picked[7], 3)]
    got_z[3] = move_z(after(picked[3], got_z[1]), 3, 1)
    got_x[2] = move_x(after(picked[6], got_x[1]), 2)
    got_z[0] = move_z(after(picked[0], got_z[2]), 0, 1)
    mine_f, mine_n = second(got_x, move_z)
    recv_f, recv_n = second(got_z, move_x)
    source = (x - dx + NX) % NX * NZ + (z - move + NZ) % NZ
    base = ctx * (NX * NZ * LANES) + source * LANES

    def scalars(far):
        want = 2 * (x * NZ + (z + far) % NZ) + role
        length = lookup(request_decode_slot, lengths, want)
        return jnp.concatenate([(length - base).reshape(-1), role[None], ctx[None]]).astype(jnp.int32)

    q_nope = after(q_nope, picked[1])
    queries = q_nope.reshape(req_dev, steps, heads_dev, nope_dim)
    absorbed = jnp.einsum("bshd,hdk->bshk", queries, w_key, preferred_element_type=jnp.float32).astype(jnp.bfloat16)
    own = jnp.concatenate([absorbed, q_rope.reshape(req_dev, steps, heads_dev, rope_dim)], axis=3)
    both = jnp.stack([own, move_far(own)], axis=1)
    keep = jnp.where(role == 0, both[0], both[1])
    got = swap_role(jnp.where(role == 0, both[1], both[0]))
    pair = jnp.stack([jnp.where(role == 0, keep, got), jnp.where(role == 0, got, keep)], axis=1)
    every = lax.all_gather(pair, "ctx", axis=2, tiled=False)
    every = every.reshape(2, -1, latent + rope_dim)

    part_f = attend(scalars(4), after(every[1], (mine_n[1], recv_n[1])), mine_f, recv_f, None, latent, scale)
    heads = 2 * lax.axis_size("ctx")
    part_f = lax.all_to_all(part_f.reshape(heads, -1, latent + LANES), ("role", "ctx"), 0, 0, tiled=True)
    rows_f, lse_f = merge(part_f.reshape(2, -1, *part_f.shape[1:]), latent, 1)
    packed = jnp.concatenate(
        [rows_f.astype(jnp.bfloat16), pack_columns(lse_f, lax.broadcasted_iota(jnp.int32, (*lse_f.shape[:2], LANES), 2))], axis=-1)
    packed = move_far(packed)

    new = jnp.where(role == 0, new_latent[0], new_latent[1])
    new = jnp.pad(new.T, ((0, 0), (0, LANES - steps)))
    part_n = attend(scalars(0), every[0], mine_n, recv_n, new, latent, scale)
    part_n = lax.all_to_all(part_n.reshape(heads, -1, latent + LANES), ("role", "ctx"), 0, 0, tiled=True)
    parts = jnp.concatenate([part_n.reshape(2, -1, *part_n.shape[1:]), packed[:, None]], axis=1)
    merged, _ = merge(parts, latent, 1)
    merged = merged.astype(jnp.bfloat16).reshape(req_dev, steps, heads_dev, latent)
    out = jnp.einsum("bshk,hkv->bshv", merged, value_up_weight, preferred_element_type=jnp.float32).astype(jnp.bfloat16)
    return out.reshape(req_dev, steps, -1)


def solution(mesh):
    placed = (
        P(None, ("ctx", "req"), "role"),
        P(),
        P(),
        P("req", None, ("role", "ctx")),
        P("req", None, ("role", "ctx")),
        P("req", None, None),
        P(("role", "ctx"), None, None),
        P(("role", "ctx"), None, None),
    )
    return jax.shard_map(
        shards,
        mesh=mesh,
        in_specs=placed,
        out_specs=P("req", None, ("role", "ctx")),
        check_vma=False,
    )
```

```python
import functools

import jax
import jax.numpy as jnp
from jax import lax
from jax.experimental import pallas as pl
from jax.experimental.pallas import tpu as pltpu
from jax.sharding import PartitionSpec as P

NX, NZ = 4, 8
NC = 4
LANES = 128
NEG = -1e30


def z_to(z, c):
    return (z + (0, 1, -1, 2 if z % 2 == 0 else -2)[c]) % NZ


def move_z(a, c, flip=0):
    if c == 0 and not flip:
        return a
    n = NX * NZ
    pairs = [(r * n + x * NZ + z, (r ^ flip) * n + x * NZ + z_to(z, c)) for r in range(2) for x in range(NX) for z in range(NZ)]
    return lax.ppermute(a, ("role", "req"), pairs)


def move_x(a, dx):
    if dx == 0:
        return a
    return lax.ppermute(a, "req", [(x * NZ + z, (x + dx) % NX * NZ + z) for x in range(NX) for z in range(NZ)])


def move_far(a):
    return lax.ppermute(a, "req", [(x * NZ + z, x * NZ + (z + 4) % NZ) for x in range(NX) for z in range(NZ)])


def swap_role(a):
    return lax.ppermute(a, "role", [(0, 1), (1, 0)])


def lookup(slots, values, want):
    return jnp.max(jnp.where(slots == want[..., None], values, 0), axis=-1)


def pick_kernel(idx_ref, k_ref, *outs):
    for o, out in enumerate(outs):
        for g in range(2):
            for i in range(4):
                out[g, i] = k_ref[idx_ref[o * 8 + g * 4 + i]]


def pick(k, idx):
    vm = pl.BlockSpec(memory_space=pltpu.VMEM)
    block = k.shape[1:]
    return pl.pallas_call(
        pick_kernel,
        in_specs=[pl.BlockSpec(memory_space=pltpu.SMEM), vm],
        out_specs=[vm] * 8,
        out_shape=[pltpu.VMEM((2, 4, *block), k.dtype)] * 8,
        compiler_params=pltpu.CompilerParams(vmem_limit_bytes=12 * 1024 * 1024),
        cost_estimate=pl.CostEstimate(flops=0, bytes_accessed=2 * 64 * block[0] * block[1] * 2, transcendentals=0),
    )(idx, k)


def regroup_kernel(*refs):
    for g in range(2):
        for i in range(4):
            for j in range(4):
                refs[4 + g * 4 + i][j] = refs[j][g, i]


def regroup(parts):
    vm = pl.BlockSpec(memory_space=pltpu.VMEM)
    shape = parts[0].shape[1:]
    size = shape[0] * shape[1] * shape[2]
    return pl.pallas_call(
        regroup_kernel,
        in_specs=[vm] * 4,
        out_specs=[vm] * 8,
        out_shape=[pltpu.VMEM(shape, parts[0].dtype)] * 8,
        compiler_params=pltpu.CompilerParams(vmem_limit_bytes=8 * 1024 * 1024),
        cost_estimate=pl.CostEstimate(flops=0, bytes_accessed=2 * 8 * size * 2, transcendentals=0),
    )(*parts)


def attend_kernel(fresh, scale, scal_ref, q_ref, *rest):
    mine, recv = rest[:4], rest[4:8]
    rest = rest[8:]
    if fresh:
        new_ref, rest = rest[0], rest[1:]
    o_ref, kt, s_ref = rest
    half = mine[0].shape[1]
    latent = o_ref.shape[1] - LANES
    rows = q_ref.shape[0]
    role = scal_ref[16]
    at_mine = pl.ds(pl.multiple_of(role * half, 32), half)
    at_recv = pl.ds(pl.multiple_of((1 - role) * half, 32), half)
    chunk = 4 * LANES
    lane = lax.broadcasted_iota(jnp.int32, (1, LANES), 1)
    high = jnp.full((rows, LANES), NEG, jnp.float32)
    for j in range(4):
        for c in range(4):
            cols = slice(j * chunk + c * LANES, j * chunk + (c + 1) * LANES)
            kt[at_mine, cols] = mine[c][j]
            kt[at_recv, cols] = recv[j][c]
        s = jnp.dot(q_ref[...], kt[:, j * chunk:(j + 1) * chunk], preferred_element_type=jnp.float32)
        for c in range(4):
            t = s[:, c * LANES:(c + 1) * LANES] * scale
            t = jnp.where(lane < scal_ref[j * 4 + c], t, NEG)
            s_ref[:, j * chunk + c * LANES:j * chunk + (c + 1) * LANES] = t
            high = jnp.maximum(high, t)
    if fresh:
        t = jnp.dot(q_ref[...], new_ref[...], preferred_element_type=jnp.float32) * scale
        step = (lax.broadcasted_iota(jnp.int32, (rows, LANES), 0) // 16) % 4
        u = lax.broadcasted_iota(jnp.int32, (rows, LANES), 1)
        f = jnp.where((u <= step) & (scal_ref[17] == 0), t, NEG)
        high = jnp.maximum(high, f)
    m = jnp.maximum(jnp.max(high, axis=1, keepdims=True), -1e29)
    total = jnp.zeros((rows, LANES), jnp.float32)
    acc = jnp.zeros((rows, latent), jnp.float32)
    nt = (((1,), (1,)), ((), ()))
    for j in range(4):
        w = jnp.exp(s_ref[:, j * chunk:(j + 1) * chunk] - m)
        for c in range(4):
            total = total + w[:, c * LANES:(c + 1) * LANES]
        acc = acc + lax.dot_general(w.astype(jnp.bfloat16), kt[:latent, j * chunk:(j + 1) * chunk], nt,
                                    preferred_element_type=jnp.float32)
    if fresh:
        w = jnp.exp(f - m)
        total = total + w
        acc = acc + lax.dot_general(w.astype(jnp.bfloat16), new_ref[:latent, :], nt, preferred_element_type=jnp.float32)
    norm = jnp.sum(total, axis=1, keepdims=True)
    some = norm > 0.0
    safe = jnp.where(some, norm, 1.0)
    o_ref[:, :latent] = (acc / safe).astype(jnp.bfloat16)
    lse = jnp.where(some, m + jnp.log(safe), NEG)
    o_ref[:, latent:] = pack_columns(lse, lax.broadcasted_iota(jnp.int32, (rows, LANES), 1))


def pack_columns(lse, lane):
    a = lse.astype(jnp.bfloat16).astype(jnp.float32)
    b = (lse - a).astype(jnp.bfloat16).astype(jnp.float32)
    c = (lse - a) - b
    return jnp.where(lane == 0, a, jnp.where(lane == 1, b, jnp.where(lane == 2, c, 0.0))).astype(jnp.bfloat16)


def attend(scal, q, mine, recv, new, latent, scale):
    rows, width = q.shape
    fresh = new is not None
    vm = pl.BlockSpec(memory_space=pltpu.VMEM)
    args = [q, *mine, *recv] + ([new] if fresh else [])
    positions = 16 * LANES
    return pl.pallas_call(
        functools.partial(attend_kernel, fresh, scale),
        in_specs=[pl.BlockSpec(memory_space=pltpu.SMEM)] + [vm] * len(args),
        out_specs=vm,
        out_shape=jax.ShapeDtypeStruct((rows, latent + LANES), jnp.bfloat16),
        scratch_shapes=[pltpu.VMEM((width, positions), jnp.bfloat16), pltpu.VMEM((rows, positions), jnp.float32)],
        compiler_params=pltpu.CompilerParams(vmem_limit_bytes=20 * 1024 * 1024),
        cost_estimate=pl.CostEstimate(flops=16 * rows * positions * (width + latent),
                                      bytes_accessed=positions * width * 2 + rows * (width + latent) * 2,
                                      transcendentals=rows * positions),
    )(scal, *args)


def merge(parts, latent, axis):
    lse = jnp.sum(parts[..., latent:latent + 3].astype(jnp.float32), axis=-1, keepdims=True)
    top = jnp.max(lse, axis=axis, keepdims=True)
    w = jnp.exp(lse - top)
    norm = jnp.sum(w, axis=axis)
    rows = jnp.sum(parts[..., :latent].astype(jnp.float32) * w, axis=axis) / norm
    return rows, jnp.squeeze(top, axis) + jnp.log(norm)


def after(v, dep):
    return lax.optimization_barrier((v, dep))[0]


def second(parts, move):
    parts = regroup(parts)
    far = [move(parts[i], i) for i in range(4)]
    near = [move(after(parts[4 + i], far[i]), i) for i in range(4)]
    return far, near


def shards(cache, lengths, request_decode_slot, q_nope, q_rope, new_latent, w_key, value_up_weight):
    heads_dev, nope_dim, latent = w_key.shape
    req_dev, steps = q_nope.shape[:2]
    rope_dim = q_rope.shape[2] // heads_dev
    scale = (nope_dim + rope_dim) ** -0.5
    role, ctx, req = lax.axis_index("role"), lax.axis_index("ctx"), lax.axis_index("req")
    x, z = req // NZ, req % NZ
    total = request_decode_slot.shape[0]
    ids = jnp.arange(total, dtype=jnp.int32)
    dx = jnp.arange(NX, dtype=jnp.int32)[:, None]
    cls = jnp.arange(NC, dtype=jnp.int32)
    move = jnp.where(cls == 1, 1, jnp.where(cls == 2, -1, jnp.where(cls == 3, jnp.where(z % 2 == 0, 2, -2), 0)))[None, :]
    blocks = jnp.swapaxes(cache, 1, 2)

    far = jnp.array([4, 0], jnp.int32)[:, None, None]
    owner = (x + dx) % NX * NZ + (z + move + far + NZ) % NZ
    take_x = lookup(request_decode_slot, ids, 2 * owner + role)
    take_z = lookup(request_decode_slot, ids, 2 * owner + 1 - role)
    index = jnp.concatenate([jnp.moveaxis(take_z, 2, 0).reshape(-1), jnp.moveaxis(take_x, 1, 0).reshape(-1)])
    picked = pick(blocks, index)
    q_nope = after(q_nope, picked[1])
    queries = q_nope.reshape(req_dev, steps, heads_dev, nope_dim)
    absorbed = jnp.einsum("bshd,hdk->bshk", queries, w_key, preferred_element_type=jnp.float32).astype(jnp.bfloat16)
    own = jnp.concatenate([absorbed, q_rope.reshape(req_dev, steps, heads_dev, rope_dim)], axis=3)

    got_x = [move_x(picked[4 + i], i) for i in range(4)]
    got_z = [move_z(picked[i], i, 1) for i in range(4)]
    got_x, got_z, both = lax.optimization_barrier((got_x, got_z, (own, move_far(own))))
    both = jnp.stack(both, axis=1)
    heads = 2 * lax.axis_size("ctx")
    spread = jnp.broadcast_to(both[:, None], (req_dev, lax.axis_size("ctx"), *both.shape[1:]))
    every = lax.all_to_all(spread.reshape(heads, *both.shape[1:]), ("role", "ctx"), 0, 0, tiled=True)
    every = jnp.moveaxis(every, 1, 0).reshape(2, -1, latent + rope_dim)
    mine_f, mine_n = second(got_x, move_z)
    recv_f, recv_n = second(got_z, move_x)
    source = (x - dx + NX) % NX * NZ + (z - move + NZ) % NZ
    base = ctx * (NX * NZ * LANES) + source * LANES

    def scalars(far):
        want = 2 * (x * NZ + (z + far) % NZ) + role
        length = lookup(request_decode_slot, lengths, want)
        return jnp.concatenate([(length - base).reshape(-1), role[None], ctx[None]]).astype(jnp.int32)

    part_f = attend(scalars(4), every[1], mine_f, recv_f, None, latent, scale)
    part_f = lax.all_to_all(part_f.reshape(heads, -1, latent + LANES), ("role", "ctx"), 0, 0, tiled=True)
    rows_f, lse_f = merge(part_f.reshape(2, -1, *part_f.shape[1:]), latent, 1)
    packed = jnp.concatenate(
        [rows_f.astype(jnp.bfloat16), pack_columns(lse_f, lax.broadcasted_iota(jnp.int32, (*lse_f.shape[:2], LANES), 2))], axis=-1)
    packed = move_far(packed)

    new = jnp.where(role == 0, new_latent[0], new_latent[1])
    new = jnp.pad(new.T, ((0, 0), (0, LANES - steps)))
    part_n = attend(scalars(0), every[0], mine_n, recv_n, new, latent, scale)
    part_n = lax.all_to_all(part_n.reshape(heads, -1, latent + LANES), ("role", "ctx"), 0, 0, tiled=True)
    parts = jnp.concatenate([part_n.reshape(2, -1, *part_n.shape[1:]), packed[:, None]], axis=1)
    merged, _ = merge(parts, latent, 1)
    merged = merged.astype(jnp.bfloat16).reshape(req_dev, steps, heads_dev, latent)
    out = jnp.einsum("bshk,hkv->bshv", merged, value_up_weight, preferred_element_type=jnp.float32).astype(jnp.bfloat16)
    return out.reshape(req_dev, steps, -1)


def solution(mesh):
    placed = (
        P(None, ("ctx", "req"), "role"),
        P(),
        P(),
        P("req", None, ("role", "ctx")),
        P("req", None, ("role", "ctx")),
        P("req", None, None),
        P(("role", "ctx"), None, None),
        P(("role", "ctx"), None, None),
    )
    return jax.shard_map(
        shards,
        mesh=mesh,
        in_specs=placed,
        out_specs=P("req", None, ("role", "ctx")),
        check_vma=False,
    )
```

```python
import functools

import jax
import jax.numpy as jnp
from jax import lax
from jax.experimental import pallas as pl
from jax.experimental.pallas import tpu as pltpu
from jax.sharding import PartitionSpec as P

NX, NZ = 4, 8
NC = 4
LANES = 128
NEG = -1e30


def z_to(z, c):
    return (z + (0, 1, -1, 2 if z % 2 == 0 else -2)[c]) % NZ


def move_z(a, c, flip=0):
    if c == 0 and not flip:
        return a
    n = NX * NZ
    pairs = [(r * n + x * NZ + z, (r ^ flip) * n + x * NZ + z_to(z, c)) for r in range(2) for x in range(NX) for z in range(NZ)]
    return lax.ppermute(a, ("role", "req"), pairs)


def move_x(a, dx):
    if dx == 0:
        return a
    return lax.ppermute(a, "req", [(x * NZ + z, (x + dx) % NX * NZ + z) for x in range(NX) for z in range(NZ)])


def move_far(a):
    return lax.ppermute(a, "req", [(x * NZ + z, x * NZ + (z + 4) % NZ) for x in range(NX) for z in range(NZ)])


def swap_role(a):
    return lax.ppermute(a, "role", [(0, 1), (1, 0)])


def lookup(slots, values, want):
    return jnp.max(jnp.where(slots == want[..., None], values, 0), axis=-1)


def pick_kernel(idx_ref, k_ref, *outs):
    for o, out in enumerate(outs):
        for g in range(2):
            for i in range(4):
                out[g, i] = k_ref[idx_ref[o * 8 + g * 4 + i]]


def pick(k, idx):
    vm = pl.BlockSpec(memory_space=pltpu.VMEM)
    block = k.shape[1:]
    return pl.pallas_call(
        pick_kernel,
        in_specs=[pl.BlockSpec(memory_space=pltpu.SMEM), vm],
        out_specs=[vm] * 8,
        out_shape=[pltpu.VMEM((2, 4, *block), k.dtype)] * 8,
        compiler_params=pltpu.CompilerParams(vmem_limit_bytes=12 * 1024 * 1024),
        cost_estimate=pl.CostEstimate(flops=0, bytes_accessed=2 * 64 * block[0] * block[1] * 2, transcendentals=0),
    )(idx, k)


def regroup_kernel(*refs):
    for g in range(2):
        for i in range(4):
            for j in range(4):
                refs[4 + g * 4 + i][j] = refs[j][g, i]


def regroup(parts):
    vm = pl.BlockSpec(memory_space=pltpu.VMEM)
    shape = parts[0].shape[1:]
    size = shape[0] * shape[1] * shape[2]
    return pl.pallas_call(
        regroup_kernel,
        in_specs=[vm] * 4,
        out_specs=[vm] * 8,
        out_shape=[pltpu.VMEM(shape, parts[0].dtype)] * 8,
        compiler_params=pltpu.CompilerParams(vmem_limit_bytes=8 * 1024 * 1024),
        cost_estimate=pl.CostEstimate(flops=0, bytes_accessed=2 * 8 * size * 2, transcendentals=0),
    )(*parts)


def attend_kernel(fresh, scale, scal_ref, q_ref, *rest):
    mine, recv = rest[:4], rest[4:8]
    rest = rest[8:]
    if fresh:
        new_ref, rest = rest[0], rest[1:]
    o_ref, kt, s_ref = rest
    half = mine[0].shape[1]
    latent = o_ref.shape[1] - LANES
    rows = q_ref.shape[0]
    role = scal_ref[16]
    at_mine = pl.ds(pl.multiple_of(role * half, 32), half)
    at_recv = pl.ds(pl.multiple_of((1 - role) * half, 32), half)
    chunk = 4 * LANES
    lane = lax.broadcasted_iota(jnp.int32, (1, LANES), 1)
    high = jnp.full((rows, LANES), NEG, jnp.float32)
    for j in range(4):
        for c in range(4):
            cols = slice(j * chunk + c * LANES, j * chunk + (c + 1) * LANES)
            kt[at_mine, cols] = mine[c][j]
            kt[at_recv, cols] = recv[j][c]
        s = jnp.dot(q_ref[...], kt[:, j * chunk:(j + 1) * chunk], preferred_element_type=jnp.float32)
        for c in range(4):
            t = s[:, c * LANES:(c + 1) * LANES] * scale
            t = jnp.where(lane < scal_ref[j * 4 + c], t, NEG)
            s_ref[:, j * chunk + c * LANES:j * chunk + (c + 1) * LANES] = t
            high = jnp.maximum(high, t)
    if fresh:
        t = jnp.dot(q_ref[...], new_ref[...], preferred_element_type=jnp.float32) * scale
        step = (lax.broadcasted_iota(jnp.int32, (rows, LANES), 0) // 16) % 4
        u = lax.broadcasted_iota(jnp.int32, (rows, LANES), 1)
        f = jnp.where((u <= step) & (scal_ref[17] == 0), t, NEG)
        high = jnp.maximum(high, f)
    m = jnp.maximum(jnp.max(high, axis=1, keepdims=True), -1e29)
    total = jnp.zeros((rows, LANES), jnp.float32)
    acc = jnp.zeros((rows, latent), jnp.float32)
    nt = (((1,), (1,)), ((), ()))
    for j in range(4):
        w = jnp.exp(s_ref[:, j * chunk:(j + 1) * chunk] - m)
        for c in range(4):
            total = total + w[:, c * LANES:(c + 1) * LANES]
        acc = acc + lax.dot_general(w.astype(jnp.bfloat16), kt[:latent, j * chunk:(j + 1) * chunk], nt,
                                    preferred_element_type=jnp.float32)
    if fresh:
        w = jnp.exp(f - m)
        total = total + w
        acc = acc + lax.dot_general(w.astype(jnp.bfloat16), new_ref[:latent, :], nt, preferred_element_type=jnp.float32)
    norm = jnp.sum(total, axis=1, keepdims=True)
    some = norm > 0.0
    safe = jnp.where(some, norm, 1.0)
    o_ref[:, :latent] = (acc / safe).astype(jnp.bfloat16)
    lse = jnp.where(some, m + jnp.log(safe), NEG)
    o_ref[:, latent:] = pack_columns(lse, lax.broadcasted_iota(jnp.int32, (rows, LANES), 1))


def pack_columns(lse, lane):
    a = lse.astype(jnp.bfloat16).astype(jnp.float32)
    b = (lse - a).astype(jnp.bfloat16).astype(jnp.float32)
    c = (lse - a) - b
    return jnp.where(lane == 0, a, jnp.where(lane == 1, b, jnp.where(lane == 2, c, 0.0))).astype(jnp.bfloat16)


def attend(scal, q, mine, recv, new, latent, scale):
    rows, width = q.shape
    fresh = new is not None
    vm = pl.BlockSpec(memory_space=pltpu.VMEM)
    args = [q, *mine, *recv] + ([new] if fresh else [])
    positions = 16 * LANES
    return pl.pallas_call(
        functools.partial(attend_kernel, fresh, scale),
        in_specs=[pl.BlockSpec(memory_space=pltpu.SMEM)] + [vm] * len(args),
        out_specs=vm,
        out_shape=jax.ShapeDtypeStruct((rows, latent + LANES), jnp.bfloat16),
        scratch_shapes=[pltpu.VMEM((width, positions), jnp.bfloat16), pltpu.VMEM((rows, positions), jnp.float32)],
        compiler_params=pltpu.CompilerParams(vmem_limit_bytes=20 * 1024 * 1024),
        cost_estimate=pl.CostEstimate(flops=16 * rows * positions * (width + latent),
                                      bytes_accessed=positions * width * 2 + rows * (width + latent) * 2,
                                      transcendentals=rows * positions),
    )(scal, *args)


def merge(parts, latent, axis):
    lse = jnp.sum(parts[..., latent:latent + 3].astype(jnp.float32), axis=-1, keepdims=True)
    top = jnp.max(lse, axis=axis, keepdims=True)
    w = jnp.exp(lse - top)
    norm = jnp.sum(w, axis=axis)
    rows = jnp.sum(parts[..., :latent].astype(jnp.float32) * w, axis=axis) / norm
    return rows, jnp.squeeze(top, axis) + jnp.log(norm)


def after(v, dep):
    return lax.optimization_barrier((v, dep))[0]


def second(parts, move):
    parts = regroup(parts)
    far = [move(parts[i], i) for i in range(4)]
    near = [move(after(parts[4 + i], far[i]), i) for i in range(4)]
    return far, near


def shards(cache, lengths, request_decode_slot, q_nope, q_rope, new_latent, w_key, value_up_weight):
    heads_dev, nope_dim, latent = w_key.shape
    req_dev, steps = q_nope.shape[:2]
    rope_dim = q_rope.shape[2] // heads_dev
    scale = (nope_dim + rope_dim) ** -0.5
    role, ctx, req = lax.axis_index("role"), lax.axis_index("ctx"), lax.axis_index("req")
    x, z = req // NZ, req % NZ
    total = request_decode_slot.shape[0]
    ids = jnp.arange(total, dtype=jnp.int32)
    dx = jnp.arange(NX, dtype=jnp.int32)[:, None]
    cls = jnp.arange(NC, dtype=jnp.int32)
    move = jnp.where(cls == 1, 1, jnp.where(cls == 2, -1, jnp.where(cls == 3, jnp.where(z % 2 == 0, 2, -2), 0)))[None, :]
    blocks = jnp.swapaxes(cache, 1, 2)

    far = jnp.array([4, 0], jnp.int32)[:, None, None]
    owner = (x + dx) % NX * NZ + (z + move + far + NZ) % NZ
    take_x = lookup(request_decode_slot, ids, 2 * owner + role)
    take_z = lookup(request_decode_slot, ids, 2 * owner + 1 - role)
    index = jnp.concatenate([jnp.moveaxis(take_z, 2, 0).reshape(-1), jnp.moveaxis(take_x, 1, 0).reshape(-1)])
    picked = pick(blocks, index)
    queries = q_nope.reshape(req_dev, steps, heads_dev, nope_dim)
    absorbed = jnp.einsum("bshd,hdk->bshk", queries, w_key, preferred_element_type=jnp.float32).astype(jnp.bfloat16)
    own = jnp.concatenate([absorbed, q_rope.reshape(req_dev, steps, heads_dev, rope_dim)], axis=3)

    picked, both = lax.optimization_barrier((picked, (own, move_far(own))))
    both = jnp.stack(both, axis=1)
    heads = 2 * lax.axis_size("ctx")
    spread = jnp.broadcast_to(both[:, None], (req_dev, lax.axis_size("ctx"), *both.shape[1:]))
    every = lax.all_to_all(spread.reshape(heads, *both.shape[1:]), ("role", "ctx"), 0, 0, tiled=True)
    first = [move_z(picked[1], 1, 1), move_x(picked[5], 1), move_z(picked[2], 2, 1), move_x(picked[7], 3),
             move_z(picked[3], 3, 1), move_x(picked[6], 2), move_z(picked[0], 0, 1)]
    first, every = lax.optimization_barrier((first, every))
    got_z = [first[6], first[0], first[2], first[4]]
    got_x = [picked[4], first[1], first[5], first[3]]
    every = jnp.moveaxis(every, 1, 0).reshape(2, -1, latent + rope_dim)
    mine_f, mine_n = second(got_x, move_z)
    recv_f, recv_n = second(got_z, move_x)
    source = (x - dx + NX) % NX * NZ + (z - move + NZ) % NZ
    base = ctx * (NX * NZ * LANES) + source * LANES

    def scalars(far):
        want = 2 * (x * NZ + (z + far) % NZ) + role
        length = lookup(request_decode_slot, lengths, want)
        return jnp.concatenate([(length - base).reshape(-1), role[None], ctx[None]]).astype(jnp.int32)

    part_f = attend(scalars(4), every[1], mine_f, recv_f, None, latent, scale)
    part_f = lax.all_to_all(part_f.reshape(heads, -1, latent + LANES), ("role", "ctx"), 0, 0, tiled=True)
    rows_f, lse_f = merge(part_f.reshape(2, -1, *part_f.shape[1:]), latent, 1)
    packed = jnp.concatenate(
        [rows_f.astype(jnp.bfloat16), pack_columns(lse_f, lax.broadcasted_iota(jnp.int32, (*lse_f.shape[:2], LANES), 2))], axis=-1)
    packed = move_far(packed)

    new = jnp.where(role == 0, new_latent[0], new_latent[1])
    new = jnp.pad(new.T, ((0, 0), (0, LANES - steps)))
    part_n = attend(scalars(0), every[0], mine_n, recv_n, new, latent, scale)
    part_n = lax.all_to_all(part_n.reshape(heads, -1, latent + LANES), ("role", "ctx"), 0, 0, tiled=True)
    parts = jnp.concatenate([part_n.reshape(2, -1, *part_n.shape[1:]), packed[:, None]], axis=1)
    merged, _ = merge(parts, latent, 1)
    merged = merged.astype(jnp.bfloat16).reshape(req_dev, steps, heads_dev, latent)
    out = jnp.einsum("bshk,hkv->bshv", merged, value_up_weight, preferred_element_type=jnp.float32).astype(jnp.bfloat16)
    return out.reshape(req_dev, steps, -1)


def solution(mesh):
    placed = (
        P(None, ("ctx", "req"), "role"),
        P(),
        P(),
        P("req", None, ("role", "ctx")),
        P("req", None, ("role", "ctx")),
        P("req", None, None),
        P(("role", "ctx"), None, None),
        P(("role", "ctx"), None, None),
    )
    return jax.shard_map(
        shards,
        mesh=mesh,
        in_specs=placed,
        out_specs=P("req", None, ("role", "ctx")),
        check_vma=False,
    )
```

```python
import functools

import jax
import jax.numpy as jnp
from jax import lax
from jax.experimental import pallas as pl
from jax.experimental.pallas import tpu as pltpu
from jax.sharding import PartitionSpec as P

NX, NZ = 4, 8
NC = 4
LANES = 128
NEG = -1e30


def z_to(z, c):
    return (z + (0, 1, -1, 2 if z % 2 == 0 else -2)[c]) % NZ


def move_z(a, c, flip=0):
    if c == 0 and not flip:
        return a
    n = NX * NZ
    pairs = [(r * n + x * NZ + z, (r ^ flip) * n + x * NZ + z_to(z, c)) for r in range(2) for x in range(NX) for z in range(NZ)]
    return lax.ppermute(a, ("role", "req"), pairs)


def move_x(a, dx):
    if dx == 0:
        return a
    return lax.ppermute(a, "req", [(x * NZ + z, (x + dx) % NX * NZ + z) for x in range(NX) for z in range(NZ)])


def move_far(a):
    return lax.ppermute(a, "req", [(x * NZ + z, x * NZ + (z + 4) % NZ) for x in range(NX) for z in range(NZ)])


def swap_role(a):
    return lax.ppermute(a, "role", [(0, 1), (1, 0)])


def lookup(slots, values, want):
    return jnp.max(jnp.where(slots == jnp.expand_dims(want, -1), values, 0), axis=-1)


def pick_kernel(idx_ref, k_ref, *outs):
    for o, out in enumerate(outs):
        for g in range(2):
            for i in range(4):
                out[g, i] = k_ref[idx_ref[o * 8 + g * 4 + i]]


def pick(k, idx):
    vm = pl.BlockSpec(memory_space=pltpu.VMEM)
    block = k.shape[1:]
    return pl.pallas_call(
        pick_kernel,
        in_specs=[pl.BlockSpec(memory_space=pltpu.SMEM), vm],
        out_specs=[vm] * 8,
        out_shape=[pltpu.HBM((2, 4, *block), k.dtype)] * 8,
        compiler_params=pltpu.CompilerParams(vmem_limit_bytes=12 * 1024 * 1024),
        cost_estimate=pl.CostEstimate(flops=0, bytes_accessed=2 * 64 * block[0] * block[1] * 2, transcendentals=0),
    )(idx, k)


def regroup_kernel(*refs):
    for g in range(2):
        for i in range(4):
            for j in range(4):
                refs[4 + g * 4 + i][j] = refs[j][g, i]


def regroup(parts):
    vm = pl.BlockSpec(memory_space=pltpu.VMEM)
    shape = parts[0].shape[1:]
    size = shape[0] * shape[1] * shape[2]
    return pl.pallas_call(
        regroup_kernel,
        in_specs=[vm] * 4,
        out_specs=[vm] * 8,
        out_shape=[pltpu.VMEM(shape, parts[0].dtype)] * 4 + [pltpu.HBM(shape, parts[0].dtype)] * 4,
        compiler_params=pltpu.CompilerParams(vmem_limit_bytes=8 * 1024 * 1024),
        cost_estimate=pl.CostEstimate(flops=0, bytes_accessed=2 * 8 * size * 2, transcendentals=0),
    )(*parts)


def attend_kernel(fresh, scale, scal_ref, q_ref, *rest):
    mine, recv = rest[:4], rest[4:8]
    rest = rest[8:]
    if fresh:
        new_ref, rest = rest[0], rest[1:]
    o_ref, kt, s_ref = rest[:3]
    half = mine[0].shape[1]
    latent = o_ref.shape[1] - LANES
    rows = q_ref.shape[0]
    role = scal_ref[16]
    at_mine = pl.ds(pl.multiple_of(role * half, 32), half)
    at_recv = pl.ds(pl.multiple_of((1 - role) * half, 32), half)
    chunk = 4 * LANES
    lane = lax.broadcasted_iota(jnp.int32, (1, LANES), 1)
    nt = (((1,), (1,)), ((), ()))
    high = jnp.full((rows, LANES), NEG, jnp.float32)
    copies = []
    if fresh:
        sems = rest[3]
        for j in range(4):
            for c in range(4):
                cols, n = pl.ds(j * chunk + c * LANES, LANES), 8 * j + 2 * c
                copies.append(pltpu.make_async_copy(mine[c].at[j], kt.at[at_mine, cols], sems.at[n]))
                copies.append(pltpu.make_async_copy(recv[j].at[c], kt.at[at_recv, cols], sems.at[n + 1]))
        for copy in copies:
            copy.start()
    for j in range(4):
        for copy in copies[8 * j:8 * j + 8]:
            copy.wait()
        if not fresh:
            for c in range(4):
                cols = slice(j * chunk + c * LANES, j * chunk + (c + 1) * LANES)
                kt[at_mine, cols] = mine[c][j]
                kt[at_recv, cols] = recv[j][c]
        s = jnp.dot(q_ref[...], kt[:, j * chunk:(j + 1) * chunk], preferred_element_type=jnp.float32)
        for c in range(4):
            t = s[:, c * LANES:(c + 1) * LANES] * scale
            t = jnp.where(lane < scal_ref[j * 4 + c], t, NEG)
            s_ref[:, j * chunk + c * LANES:j * chunk + (c + 1) * LANES] = t
            high = jnp.maximum(high, t)
    if fresh:
        t = lax.dot_general(q_ref[...], new_ref[...], nt, preferred_element_type=jnp.float32) * scale
        step = (lax.broadcasted_iota(jnp.int32, (rows, LANES), 0) // 16) % 4
        u = lax.broadcasted_iota(jnp.int32, (rows, LANES), 1)
        f = jnp.where((u <= step) & (scal_ref[17] == 0), t, NEG)
        high = jnp.maximum(high, f)
    m = jnp.maximum(jnp.max(high, axis=1, keepdims=True), -1e29)
    total = jnp.zeros((rows, LANES), jnp.float32)
    acc = jnp.zeros((rows, latent), jnp.float32)
    for j in range(4):
        w = jnp.exp(s_ref[:, j * chunk:(j + 1) * chunk] - m)
        for c in range(4):
            total = total + w[:, c * LANES:(c + 1) * LANES]
        acc = acc + lax.dot_general(w.astype(jnp.bfloat16), kt[:latent, j * chunk:(j + 1) * chunk], nt,
                                    preferred_element_type=jnp.float32)
    if fresh:
        w = jnp.exp(f - m)
        total = total + w
        acc = acc + jnp.dot(w.astype(jnp.bfloat16), new_ref[:, :latent], preferred_element_type=jnp.float32)
    norm = jnp.sum(total, axis=1, keepdims=True)
    some = norm > 0.0
    safe = jnp.where(some, norm, 1.0)
    o_ref[:, :latent] = (acc / safe).astype(jnp.bfloat16)
    lse = jnp.where(some, m + jnp.log(safe), NEG)
    o_ref[:, latent:] = pack_columns(lse, lax.broadcasted_iota(jnp.int32, (rows, LANES), 1))


def pack_columns(lse, lane):
    a = lse.astype(jnp.bfloat16).astype(jnp.float32)
    b = (lse - a).astype(jnp.bfloat16).astype(jnp.float32)
    c = (lse - a) - b
    return jnp.where(lane == 0, a, jnp.where(lane == 1, b, jnp.where(lane == 2, c, 0.0))).astype(jnp.bfloat16)


def attend(scal, q, mine, recv, new, latent, scale):
    rows, width = q.shape
    fresh = new is not None
    vm = pl.BlockSpec(memory_space=pltpu.VMEM)
    if fresh:
        mine, recv = [[pltpu.with_memory_space_constraint(a, pltpu.HBM) for a in side] for side in (mine, recv)]
    args = [q, *mine, *recv] + ([new] if fresh else [])
    positions = 16 * LANES
    return pl.pallas_call(
        functools.partial(attend_kernel, fresh, scale),
        in_specs=[pl.BlockSpec(memory_space=pltpu.SMEM), vm] + [pl.BlockSpec(memory_space=pltpu.HBM) if fresh else vm] * 8 + [vm] * fresh,
        out_specs=vm,
        out_shape=pltpu.HBM((rows, latent + LANES), jnp.bfloat16),
        scratch_shapes=[pltpu.VMEM((width, positions), jnp.bfloat16), pltpu.VMEM((rows, positions), jnp.float32)]
        + [pltpu.SemaphoreType.DMA((32,))] * fresh,
        compiler_params=pltpu.CompilerParams(vmem_limit_bytes=20 * 1024 * 1024),
        cost_estimate=pl.CostEstimate(flops=16 * rows * positions * (width + latent),
                                      bytes_accessed=positions * width * 2 + rows * (width + latent) * 2,
                                      transcendentals=rows * positions),
    )(scal, *args)


def merge(parts, latent, axis):
    lse = jnp.sum(parts[..., latent:latent + 3].astype(jnp.float32), axis=-1, keepdims=True)
    top = jnp.max(lse, axis=axis, keepdims=True)
    w = jnp.exp(lse - top)
    norm = jnp.sum(w, axis=axis)
    rows = jnp.sum(parts[..., :latent].astype(jnp.float32) * w, axis=axis) / norm
    return rows, jnp.squeeze(top, axis) + jnp.log(norm)


def merge_kernel(parts_ref, o_ref):
    slots, rows, width = o_ref.shape
    latent = width - LANES
    count = parts_ref.shape[0] // slots
    lane = lax.broadcasted_iota(jnp.int32, (rows, LANES), 1)
    for s in range(slots):
        parts = [parts_ref[s * count + i] for i in range(count)]
        lse = [jnp.sum(jnp.where(lane < 3, p[:, latent:].astype(jnp.float32), 0.0), axis=1, keepdims=True) for p in parts]
        top = functools.reduce(jnp.maximum, lse)
        w = [jnp.exp(v - top) for v in lse]
        norm = functools.reduce(jnp.add, w)
        total = functools.reduce(jnp.add, [p[:, :latent].astype(jnp.float32) * v for p, v in zip(parts, w)])
        o_ref[s, :, :latent] = (total / norm).astype(jnp.bfloat16)
        o_ref[s, :, latent:] = pack_columns(top + jnp.log(norm), lane)


def merge_slots(parts, slots):
    vm = pl.BlockSpec(memory_space=pltpu.VMEM)
    return pl.pallas_call(
        merge_kernel,
        in_specs=[vm],
        out_specs=vm,
        out_shape=jax.ShapeDtypeStruct((slots, *parts.shape[1:]), parts.dtype),
        compiler_params=pltpu.CompilerParams(vmem_limit_bytes=8 * 1024 * 1024),
        cost_estimate=pl.CostEstimate(flops=4 * parts.size, bytes_accessed=2 * parts.size, transcendentals=1024),
    )(parts)


def after(v, dep):
    return lax.optimization_barrier((v, dep))[0]


def second(parts, move):
    parts = regroup(parts)
    far = [move(parts[i], i) for i in range(4)]
    near = [move(after(parts[4 + i], far[i]), i) for i in range(4)]
    return far, near


def shards(cache, lengths, request_decode_slot, q_nope, q_rope, new_latent, w_key, value_up_weight):
    heads_dev, nope_dim, latent = w_key.shape
    req_dev, steps = q_nope.shape[:2]
    rope_dim = q_rope.shape[2] // heads_dev
    scale = (nope_dim + rope_dim) ** -0.5
    role, ctx, req = lax.axis_index("role"), lax.axis_index("ctx"), lax.axis_index("req")
    x, z = req // NZ, req % NZ
    ids = jnp.arange(request_decode_slot.shape[0], dtype=jnp.int32)
    blocks = jnp.swapaxes(cache, 1, 2)

    def move(c):
        return jnp.where(c == 1, 1, jnp.where(c == 2, -1, jnp.where(c == 3, 2 - 4 * (z % 2), 0)))

    outer, inner, far = ids // 8, ids % 4, 4 - ids // 4 % 2 * 4
    z_first = outer < NC
    dx, cls = jnp.where(z_first, inner, outer - NC), jnp.where(z_first, outer, inner)
    owner = (x + dx) % NX * NZ + (z + move(cls) + far + NZ) % NZ
    picked = pick(blocks, lookup(request_decode_slot, ids, 2 * owner + jnp.where(z_first, 1 - role, role)))
    queries = q_nope.reshape(req_dev, steps, heads_dev, nope_dim)
    absorbed = jnp.einsum("bshd,hdk->bshk", queries, w_key, preferred_element_type=jnp.float32).astype(jnp.bfloat16)
    own = jnp.concatenate([absorbed, q_rope.reshape(req_dev, steps, heads_dev, rope_dim)], axis=3)

    picked, both = lax.optimization_barrier((picked, (own, move_far(own))))
    both = jnp.stack(both, axis=1)
    heads = 2 * lax.axis_size("ctx")
    spread = jnp.broadcast_to(both[:, None], (req_dev, lax.axis_size("ctx"), *both.shape[1:]))
    every = lax.all_to_all(spread.reshape(heads, *both.shape[1:]), ("role", "ctx"), 0, 0, tiled=True)
    first = [move_z(picked[1], 1, 1), move_x(picked[5], 1), move_z(picked[2], 2, 1), move_x(picked[7], 3),
             move_z(picked[3], 3, 1), move_x(picked[6], 2), move_z(picked[0], 0, 1)]
    first, every = lax.optimization_barrier((first, every))
    got_z = [first[6], first[0], first[2], first[4]]
    got_x = [picked[4], first[1], first[5], first[3]]
    every = jnp.moveaxis(every, 1, 0).reshape(2, -1, latent + rope_dim)
    mine_f, mine_n = second(got_x, move_z)
    recv_f, recv_n = second(got_z, move_x)
    step = jnp.arange(NX * NC, dtype=jnp.int32)
    source = (x - step // NC + NX) % NX * NZ + (z - move(step % NC) + NZ) % NZ
    base = (ctx * (NX * NZ) + source) * LANES

    def scalars(far):
        length = lookup(request_decode_slot, lengths, 2 * (x * NZ + (z + far) % NZ) + role)
        return jnp.concatenate([length - base, role[None], ctx[None]]).astype(jnp.int32)

    part_f = attend(scalars(4), every[1], mine_f, recv_f, None, latent, scale)
    part_f = lax.all_to_all(part_f.reshape(heads, -1, latent + LANES), ("role", "ctx"), 0, 0, tiled=True)
    merged_f = merge_slots(part_f, req_dev)
    packed = move_far(merged_f)

    new = jnp.where(role == 0, new_latent[0], new_latent[1])
    new = jnp.pad(new, ((0, LANES - steps), (0, 0)))
    part_n = attend(scalars(0), every[0], mine_n, recv_n, new, latent, scale)
    part_n = after(part_n, merged_f)
    part_n = lax.all_to_all(part_n.reshape(heads, -1, latent + LANES), ("role", "ctx"), 0, 0, tiled=True)
    parts = jnp.concatenate([part_n.reshape(2, -1, *part_n.shape[1:]), packed[:, None]], axis=1)
    merged, _ = merge(parts, latent, 1)
    merged = merged.astype(jnp.bfloat16).reshape(req_dev, steps, heads_dev, latent)
    out = jnp.einsum("bshk,hkv->bshv", merged, value_up_weight, preferred_element_type=jnp.float32).astype(jnp.bfloat16)
    return out.reshape(req_dev, steps, -1)


def solution(mesh):
    placed = (
        P(None, ("ctx", "req"), "role"),
        P(),
        P(),
        P("req", None, ("role", "ctx")),
        P("req", None, ("role", "ctx")),
        P("req", None, None),
        P(("role", "ctx"), None, None),
        P(("role", "ctx"), None, None),
    )
    return jax.shard_map(
        shards,
        mesh=mesh,
        in_specs=placed,
        out_specs=P("req", None, ("role", "ctx")),
        check_vma=False,
    )
```

```python
import functools

import jax
import jax.numpy as jnp
from jax import lax
from jax.experimental import pallas as pl
from jax.experimental.pallas import tpu as pltpu
from jax.sharding import PartitionSpec as P

NX, NZ = 4, 8
NC = 4
LANES = 128
NEG = -1e30


def z_to(z, c):
    return (z + (0, 1, -1, 2 if z % 2 == 0 else -2)[c]) % NZ


def move_z(a, c, flip=0):
    if c == 0 and not flip:
        return a
    n = NX * NZ
    pairs = [(r * n + x * NZ + z, (r ^ flip) * n + x * NZ + z_to(z, c)) for r in range(2) for x in range(NX) for z in range(NZ)]
    return lax.ppermute(a, ("role", "req"), pairs)


def move_x(a, dx):
    if dx == 0:
        return a
    return lax.ppermute(a, "req", [(x * NZ + z, (x + dx) % NX * NZ + z) for x in range(NX) for z in range(NZ)])


def move_far(a):
    return lax.ppermute(a, "req", [(x * NZ + z, x * NZ + (z + 4) % NZ) for x in range(NX) for z in range(NZ)])


def swap_role(a):
    return lax.ppermute(a, "role", [(0, 1), (1, 0)])


def lookup(slots, values, want):
    return jnp.max(jnp.where(slots == jnp.expand_dims(want, -1), values, 0), axis=-1)


def pick_kernel(idx_ref, k_ref, *outs):
    for o, out in enumerate(outs):
        for g in range(2):
            for i in range(4):
                out[g, i] = k_ref[idx_ref[o * 8 + g * 4 + i]]


def pick(k, idx):
    vm = pl.BlockSpec(memory_space=pltpu.VMEM)
    block = k.shape[1:]
    return pl.pallas_call(
        pick_kernel,
        in_specs=[pl.BlockSpec(memory_space=pltpu.SMEM), vm],
        out_specs=[vm] * 8,
        out_shape=[pltpu.HBM((2, 4, *block), k.dtype)] * 8,
        compiler_params=pltpu.CompilerParams(vmem_limit_bytes=12 * 1024 * 1024),
        cost_estimate=pl.CostEstimate(flops=0, bytes_accessed=2 * 64 * block[0] * block[1] * 2, transcendentals=0),
    )(idx, k)


def regroup_kernel(*refs):
    for g in range(2):
        for i in range(4):
            for j in range(4):
                refs[4 + g * 4 + i][j] = refs[j][g, i]


def regroup(parts):
    vm = pl.BlockSpec(memory_space=pltpu.VMEM)
    shape = parts[0].shape[1:]
    size = shape[0] * shape[1] * shape[2]
    return pl.pallas_call(
        regroup_kernel,
        in_specs=[vm] * 4,
        out_specs=[vm] * 8,
        out_shape=[pltpu.VMEM(shape, parts[0].dtype)] * 4 + [pltpu.HBM(shape, parts[0].dtype)] * 4,
        compiler_params=pltpu.CompilerParams(vmem_limit_bytes=8 * 1024 * 1024),
        cost_estimate=pl.CostEstimate(flops=0, bytes_accessed=2 * 8 * size * 2, transcendentals=0),
    )(*[pltpu.with_memory_space_constraint(p, pltpu.HBM) for p in parts])


def attend_kernel(fresh, scale, scal_ref, q_ref, *rest):
    mine, recv = rest[:4], rest[4:8]
    rest = rest[8:]
    if fresh:
        new_ref, rest = rest[0], rest[1:]
    o_ref, kt, s_ref = rest[:3]
    half = mine[0].shape[1]
    latent = o_ref.shape[1] - LANES
    rows = q_ref.shape[0]
    role = scal_ref[16]
    at_mine = pl.ds(pl.multiple_of(role * half, 32), half)
    at_recv = pl.ds(pl.multiple_of((1 - role) * half, 32), half)
    chunk = 4 * LANES
    lane = lax.broadcasted_iota(jnp.int32, (1, LANES), 1)
    nt = (((1,), (1,)), ((), ()))
    high = jnp.full((rows, LANES), NEG, jnp.float32)
    copies = []
    if fresh:
        sems, q_vm = rest[3:]
        copies_q = pltpu.make_async_copy(q_ref, q_vm, sems.at[32])
        copies_q.start()
        q_ref = q_vm
        for j in range(4):
            for c in range(4):
                cols, n = pl.ds(j * chunk + c * LANES, LANES), 8 * j + 2 * c
                copies.append(pltpu.make_async_copy(mine[c].at[j], kt.at[at_mine, cols], sems.at[n]))
                copies.append(pltpu.make_async_copy(recv[j].at[c], kt.at[at_recv, cols], sems.at[n + 1]))
        for copy in copies:
            copy.start()
        copies_q.wait()
    for j in range(4):
        for copy in copies[8 * j:8 * j + 8]:
            copy.wait()
        if not fresh:
            for c in range(4):
                cols = slice(j * chunk + c * LANES, j * chunk + (c + 1) * LANES)
                kt[at_mine, cols] = mine[c][j]
                kt[at_recv, cols] = recv[j][c]
        s = jnp.dot(q_ref[...], kt[:, j * chunk:(j + 1) * chunk], preferred_element_type=jnp.float32)
        for c in range(4):
            t = s[:, c * LANES:(c + 1) * LANES] * scale
            t = jnp.where(lane < scal_ref[j * 4 + c], t, NEG)
            s_ref[:, j * chunk + c * LANES:j * chunk + (c + 1) * LANES] = t
            high = jnp.maximum(high, t)
    if fresh:
        t = lax.dot_general(q_ref[...], new_ref[...], nt, preferred_element_type=jnp.float32) * scale
        step = (lax.broadcasted_iota(jnp.int32, (rows, LANES), 0) // 16) % 4
        u = lax.broadcasted_iota(jnp.int32, (rows, LANES), 1)
        f = jnp.where((u <= step) & (scal_ref[17] == 0), t, NEG)
        high = jnp.maximum(high, f)
    m = jnp.maximum(jnp.max(high, axis=1, keepdims=True), -1e29)
    total = jnp.zeros((rows, LANES), jnp.float32)
    acc = jnp.zeros((rows, latent), jnp.float32)
    for j in range(4):
        w = jnp.exp(s_ref[:, j * chunk:(j + 1) * chunk] - m)
        for c in range(4):
            total = total + w[:, c * LANES:(c + 1) * LANES]
        acc = acc + lax.dot_general(w.astype(jnp.bfloat16), kt[:latent, j * chunk:(j + 1) * chunk], nt,
                                    preferred_element_type=jnp.float32)
    if fresh:
        w = jnp.exp(f - m)
        total = total + w
        acc = acc + jnp.dot(w.astype(jnp.bfloat16), new_ref[:, :latent], preferred_element_type=jnp.float32)
    norm = jnp.sum(total, axis=1, keepdims=True)
    some = norm > 0.0
    safe = jnp.where(some, norm, 1.0)
    o_ref[:, :latent] = (acc / safe).astype(jnp.bfloat16)
    lse = jnp.where(some, m + jnp.log(safe), NEG)
    o_ref[:, latent:] = pack_columns(lse, lax.broadcasted_iota(jnp.int32, (rows, LANES), 1))


def pack_columns(lse, lane):
    a = lse.astype(jnp.bfloat16).astype(jnp.float32)
    b = (lse - a).astype(jnp.bfloat16).astype(jnp.float32)
    c = (lse - a) - b
    return jnp.where(lane == 0, a, jnp.where(lane == 1, b, jnp.where(lane == 2, c, 0.0))).astype(jnp.bfloat16)


def attend(scal, q, mine, recv, new, latent, scale):
    rows, width = q.shape
    fresh = new is not None
    vm = pl.BlockSpec(memory_space=pltpu.VMEM)
    if fresh:
        q = pltpu.with_memory_space_constraint(q, pltpu.HBM)
        mine, recv = [[pltpu.with_memory_space_constraint(a, pltpu.HBM) for a in side] for side in (mine, recv)]
    args = [q, *mine, *recv] + ([new] if fresh else [])
    positions = 16 * LANES
    return pl.pallas_call(
        functools.partial(attend_kernel, fresh, scale),
        in_specs=[pl.BlockSpec(memory_space=pltpu.SMEM)] + [pl.BlockSpec(memory_space=pltpu.HBM) if fresh else vm] * 9 + [vm] * fresh,
        out_specs=vm,
        out_shape=pltpu.HBM((rows, latent + LANES), jnp.bfloat16),
        scratch_shapes=[pltpu.VMEM((width, positions), jnp.bfloat16), pltpu.VMEM((rows, positions), jnp.float32)]
        + [pltpu.SemaphoreType.DMA((33,)), pltpu.VMEM((rows, width), jnp.bfloat16)] * fresh,
        compiler_params=pltpu.CompilerParams(vmem_limit_bytes=20 * 1024 * 1024),
        cost_estimate=pl.CostEstimate(flops=16 * rows * positions * (width + latent),
                                      bytes_accessed=positions * width * 2 + rows * (width + latent) * 2,
                                      transcendentals=rows * positions),
    )(scal, *args)


def merge(parts, latent, axis):
    lse = jnp.sum(parts[..., latent:latent + 3].astype(jnp.float32), axis=-1, keepdims=True)
    top = jnp.max(lse, axis=axis, keepdims=True)
    w = jnp.exp(lse - top)
    norm = jnp.sum(w, axis=axis)
    rows = jnp.sum(parts[..., :latent].astype(jnp.float32) * w, axis=axis) / norm
    return rows, jnp.squeeze(top, axis) + jnp.log(norm)


def merge_kernel(parts_ref, o_ref):
    slots, rows, width = o_ref.shape
    latent = width - LANES
    count = parts_ref.shape[0] // slots
    lane = lax.broadcasted_iota(jnp.int32, (rows, LANES), 1)
    for s in range(slots):
        parts = [parts_ref[s * count + i] for i in range(count)]
        lse = [jnp.sum(jnp.where(lane < 3, p[:, latent:].astype(jnp.float32), 0.0), axis=1, keepdims=True) for p in parts]
        top = functools.reduce(jnp.maximum, lse)
        w = [jnp.exp(v - top) for v in lse]
        norm = functools.reduce(jnp.add, w)
        total = functools.reduce(jnp.add, [p[:, :latent].astype(jnp.float32) * v for p, v in zip(parts, w)])
        o_ref[s, :, :latent] = (total / norm).astype(jnp.bfloat16)
        o_ref[s, :, latent:] = pack_columns(top + jnp.log(norm), lane)


def merge_slots(parts, slots):
    vm = pl.BlockSpec(memory_space=pltpu.VMEM)
    return pl.pallas_call(
        merge_kernel,
        in_specs=[vm],
        out_specs=vm,
        out_shape=jax.ShapeDtypeStruct((slots, *parts.shape[1:]), parts.dtype),
        compiler_params=pltpu.CompilerParams(vmem_limit_bytes=8 * 1024 * 1024),
        cost_estimate=pl.CostEstimate(flops=4 * parts.size, bytes_accessed=2 * parts.size, transcendentals=1024),
    )(parts)


def after(v, dep):
    return lax.optimization_barrier((v, dep))[0]


def second(parts, move):
    parts = regroup(parts)
    far = [move(parts[i], i) for i in range(4)]
    near = [move(after(parts[4 + i], far[i]), i) for i in range(4)]
    return far, near


def shards(cache, lengths, request_decode_slot, q_nope, q_rope, new_latent, w_key, value_up_weight):
    heads_dev, nope_dim, latent = w_key.shape
    req_dev, steps = q_nope.shape[:2]
    rope_dim = q_rope.shape[2] // heads_dev
    scale = (nope_dim + rope_dim) ** -0.5
    role, ctx, req = lax.axis_index("role"), lax.axis_index("ctx"), lax.axis_index("req")
    x, z = req // NZ, req % NZ
    ids = jnp.arange(request_decode_slot.shape[0], dtype=jnp.int32)
    blocks = jnp.swapaxes(cache, 1, 2)

    def move(c):
        return jnp.where(c == 1, 1, jnp.where(c == 2, -1, jnp.where(c == 3, 2 - 4 * (z % 2), 0)))

    outer, inner, far = ids // 8, ids % 4, 4 - ids // 4 % 2 * 4
    z_first = outer < NC
    dx, cls = jnp.where(z_first, inner, outer - NC), jnp.where(z_first, outer, inner)
    owner = (x + dx) % NX * NZ + (z + move(cls) + far + NZ) % NZ
    picked = pick(blocks, lookup(request_decode_slot, ids, 2 * owner + jnp.where(z_first, 1 - role, role)))
    queries = q_nope.reshape(req_dev, steps, heads_dev, nope_dim)
    absorbed = jnp.einsum("bshd,hdk->bshk", queries, w_key, preferred_element_type=jnp.float32).astype(jnp.bfloat16)
    own = jnp.concatenate([absorbed, q_rope.reshape(req_dev, steps, heads_dev, rope_dim)], axis=3)

    picked, both = lax.optimization_barrier((picked, (own, move_far(own))))
    both = jnp.stack(both, axis=1)
    heads = 2 * lax.axis_size("ctx")
    spread = jnp.broadcast_to(both[:, None], (req_dev, lax.axis_size("ctx"), *both.shape[1:]))
    every = lax.all_to_all(spread.reshape(heads, *both.shape[1:]), ("role", "ctx"), 0, 0, tiled=True)
    first = [move_z(picked[1], 1, 1), move_x(picked[5], 1), move_z(picked[2], 2, 1), move_x(picked[7], 3),
             move_z(picked[3], 3, 1), move_x(picked[6], 2), move_z(picked[0], 0, 1)]
    first, every = lax.optimization_barrier((first, every))
    got_z = [first[6], first[0], first[2], first[4]]
    got_x = [picked[4], first[1], first[5], first[3]]
    every = jnp.moveaxis(every, 1, 0).reshape(2, -1, latent + rope_dim)
    mine_f, mine_n = second(got_x, move_z)
    recv_f, recv_n = second(got_z, move_x)
    step = jnp.arange(NX * NC, dtype=jnp.int32)
    source = (x - step // NC + NX) % NX * NZ + (z - move(step % NC) + NZ) % NZ
    base = (ctx * (NX * NZ) + source) * LANES

    def scalars(far):
        length = lookup(request_decode_slot, lengths, 2 * (x * NZ + (z + far) % NZ) + role)
        return jnp.concatenate([length - base, role[None], ctx[None]]).astype(jnp.int32)

    part_f = attend(scalars(4), every[1], mine_f, recv_f, None, latent, scale)
    part_f = lax.all_to_all(part_f.reshape(heads, -1, latent + LANES), ("role", "ctx"), 0, 0, tiled=True)
    merged_f = merge_slots(part_f, req_dev)
    packed = move_far(merged_f)

    new = jnp.where(role == 0, new_latent[0], new_latent[1])
    new = jnp.pad(new, ((0, LANES - steps), (0, 0)))
    part_n = attend(scalars(0), every[0], mine_n, recv_n, new, latent, scale)
    part_n = after(part_n, merged_f)
    part_n = lax.all_to_all(part_n.reshape(heads, -1, latent + LANES), ("role", "ctx"), 0, 0, tiled=True)
    parts = jnp.concatenate([part_n.reshape(2, -1, *part_n.shape[1:]), packed[:, None]], axis=1)
    merged, _ = merge(parts, latent, 1)
    merged = merged.astype(jnp.bfloat16).reshape(req_dev, steps, heads_dev, latent)
    out = jnp.einsum("bshk,hkv->bshv", merged, value_up_weight, preferred_element_type=jnp.float32).astype(jnp.bfloat16)
    return out.reshape(req_dev, steps, -1)


def solution(mesh):
    placed = (
        P(None, ("ctx", "req"), "role"),
        P(),
        P(),
        P("req", None, ("role", "ctx")),
        P("req", None, ("role", "ctx")),
        P("req", None, None),
        P(("role", "ctx"), None, None),
        P(("role", "ctx"), None, None),
    )
    return jax.shard_map(
        shards,
        mesh=mesh,
        in_specs=placed,
        out_specs=P("req", None, ("role", "ctx")),
        check_vma=False,
    )
```

```python
import functools

import jax
import jax.numpy as jnp
from jax import lax
from jax.experimental import pallas as pl
from jax.experimental.pallas import tpu as pltpu
from jax.sharding import PartitionSpec as P

NX, NZ = 4, 8
NC = 4
LANES = 128
NEG = -1e30


def z_to(z, c):
    return (z + (0, 1, -1, 2 if z % 2 == 0 else -2)[c]) % NZ


def move_z(a, c, flip=0):
    if c == 0 and not flip:
        return a
    n = NX * NZ
    pairs = [(r * n + x * NZ + z, (r ^ flip) * n + x * NZ + z_to(z, c)) for r in range(2) for x in range(NX) for z in range(NZ)]
    return lax.ppermute(a, ("role", "req"), pairs)


def move_x(a, dx):
    if dx == 0:
        return a
    return lax.ppermute(a, "req", [(x * NZ + z, (x + dx) % NX * NZ + z) for x in range(NX) for z in range(NZ)])


def move_far(a):
    return lax.ppermute(a, "req", [(x * NZ + z, x * NZ + (z + 4) % NZ) for x in range(NX) for z in range(NZ)])


def swap_role(a):
    return lax.ppermute(a, "role", [(0, 1), (1, 0)])


def lookup(slots, values, want):
    return jnp.max(jnp.where(slots == jnp.expand_dims(want, -1), values, 0), axis=-1)


def pick_kernel(idx_ref, k_ref, *outs):
    for o, out in enumerate(outs):
        for g in range(2):
            for i in range(4):
                out[g, i] = k_ref[idx_ref[o * 8 + g * 4 + i]]


def pick(k, idx):
    vm = pl.BlockSpec(memory_space=pltpu.VMEM)
    block = k.shape[1:]
    return pl.pallas_call(
        pick_kernel,
        in_specs=[pl.BlockSpec(memory_space=pltpu.SMEM), vm],
        out_specs=[vm] * 8,
        out_shape=[pltpu.HBM((2, 4, *block), k.dtype)] * 8,
        compiler_params=pltpu.CompilerParams(vmem_limit_bytes=12 * 1024 * 1024),
        cost_estimate=pl.CostEstimate(flops=0, bytes_accessed=2 * 64 * block[0] * block[1] * 2, transcendentals=0),
    )(idx, k)


def regroup_kernel(*refs):
    for g in range(2):
        for i in range(4):
            for j in range(4):
                refs[4 + g * 4 + i][j] = refs[j][g, i]


def regroup(parts):
    vm = pl.BlockSpec(memory_space=pltpu.VMEM)
    shape = parts[0].shape[1:]
    size = shape[0] * shape[1] * shape[2]
    return pl.pallas_call(
        regroup_kernel,
        in_specs=[vm] * 4,
        out_specs=[vm] * 8,
        out_shape=[pltpu.VMEM(shape, parts[0].dtype)] * 4 + [pltpu.HBM(shape, parts[0].dtype)] * 4,
        compiler_params=pltpu.CompilerParams(vmem_limit_bytes=8 * 1024 * 1024),
        cost_estimate=pl.CostEstimate(flops=0, bytes_accessed=2 * 8 * size * 2, transcendentals=0),
    )(*[pltpu.with_memory_space_constraint(p, pltpu.HBM) for p in parts])


def attend_kernel(fresh, scale, scal_ref, q_ref, *rest):
    mine, recv = rest[:4], rest[4:8]
    rest = rest[8:]
    if fresh:
        new_ref, rest = rest[0], rest[1:]
    o_ref, kt, s_ref = rest[:3]
    half = mine[0].shape[1]
    latent = o_ref.shape[1] - LANES
    rows = q_ref.shape[0]
    role = scal_ref[16]
    at_mine = pl.ds(pl.multiple_of(role * half, 32), half)
    at_recv = pl.ds(pl.multiple_of((1 - role) * half, 32), half)
    chunk = 4 * LANES
    lane = lax.broadcasted_iota(jnp.int32, (1, LANES), 1)
    nt = (((1,), (1,)), ((), ()))
    high = jnp.full((rows, LANES), NEG, jnp.float32)
    copies = []
    if fresh:
        sems, q_vm = rest[3:]
        copies_q = pltpu.make_async_copy(q_ref, q_vm, sems.at[32])
        copies_q.start()
        q_ref = q_vm
        for j in range(4):
            for c in range(4):
                cols, n = pl.ds(j * chunk + c * LANES, LANES), 8 * j + 2 * c
                copies.append(pltpu.make_async_copy(mine[c].at[j], kt.at[at_mine, cols], sems.at[n]))
                copies.append(pltpu.make_async_copy(recv[j].at[c], kt.at[at_recv, cols], sems.at[n + 1]))
        for copy in copies:
            copy.start()
        copies_q.wait()
    for j in range(4):
        for copy in copies[8 * j:8 * j + 8]:
            copy.wait()
        if not fresh:
            for c in range(4):
                cols = slice(j * chunk + c * LANES, j * chunk + (c + 1) * LANES)
                kt[at_mine, cols] = mine[c][j]
                kt[at_recv, cols] = recv[j][c]
        s = jnp.dot(q_ref[...], kt[:, j * chunk:(j + 1) * chunk], preferred_element_type=jnp.float32)
        for c in range(4):
            t = s[:, c * LANES:(c + 1) * LANES] * scale
            t = jnp.where(lane < scal_ref[j * 4 + c], t, NEG)
            s_ref[:, j * chunk + c * LANES:j * chunk + (c + 1) * LANES] = t
            high = jnp.maximum(high, t)
    if fresh:
        t = lax.dot_general(q_ref[...], new_ref[...], nt, preferred_element_type=jnp.float32) * scale
        step = (lax.broadcasted_iota(jnp.int32, (rows, LANES), 0) // 16) % 4
        u = lax.broadcasted_iota(jnp.int32, (rows, LANES), 1)
        f = jnp.where((u <= step) & (scal_ref[17] == 0), t, NEG)
        high = jnp.maximum(high, f)
    m = jnp.maximum(jnp.max(high, axis=1, keepdims=True), -1e29)
    total = jnp.zeros((rows, LANES), jnp.float32)
    acc = jnp.zeros((rows, latent), jnp.float32)
    for j in range(4):
        w = jnp.exp(s_ref[:, j * chunk:(j + 1) * chunk] - m)
        for c in range(4):
            total = total + w[:, c * LANES:(c + 1) * LANES]
        acc = acc + lax.dot_general(w.astype(jnp.bfloat16), kt[:latent, j * chunk:(j + 1) * chunk], nt,
                                    preferred_element_type=jnp.float32)
    if fresh:
        w = jnp.exp(f - m)
        total = total + w
        acc = acc + jnp.dot(w.astype(jnp.bfloat16), new_ref[:, :latent], preferred_element_type=jnp.float32)
    norm = jnp.sum(total, axis=1, keepdims=True)
    some = norm > 0.0
    safe = jnp.where(some, norm, 1.0)
    o_ref[:, :latent] = (acc / safe).astype(jnp.bfloat16)
    lse = jnp.where(some, m + jnp.log(safe), NEG)
    o_ref[:, latent:] = pack_columns(lse, lax.broadcasted_iota(jnp.int32, (rows, LANES), 1))


def pack_columns(lse, lane):
    a = lse.astype(jnp.bfloat16).astype(jnp.float32)
    b = (lse - a).astype(jnp.bfloat16).astype(jnp.float32)
    c = (lse - a) - b
    return jnp.where(lane == 0, a, jnp.where(lane == 1, b, jnp.where(lane == 2, c, 0.0))).astype(jnp.bfloat16)


def attend(scal, q, mine, recv, new, latent, scale):
    rows, width = q.shape
    fresh = new is not None
    vm = pl.BlockSpec(memory_space=pltpu.VMEM)
    if fresh:
        q = pltpu.with_memory_space_constraint(q, pltpu.HBM)
        mine, recv = [[pltpu.with_memory_space_constraint(a, pltpu.HBM) for a in side] for side in (mine, recv)]
    args = [q, *mine, *recv] + ([new] if fresh else [])
    positions = 16 * LANES
    return pl.pallas_call(
        functools.partial(attend_kernel, fresh, scale),
        in_specs=[pl.BlockSpec(memory_space=pltpu.SMEM)] + [pl.BlockSpec(memory_space=pltpu.HBM) if fresh else vm] * 9 + [vm] * fresh,
        out_specs=vm,
        out_shape=pltpu.HBM((rows, latent + LANES), jnp.bfloat16),
        scratch_shapes=[pltpu.VMEM((width, positions), jnp.bfloat16), pltpu.VMEM((rows, positions), jnp.float32)]
        + [pltpu.SemaphoreType.DMA((33,)), pltpu.VMEM((rows, width), jnp.bfloat16)] * fresh,
        compiler_params=pltpu.CompilerParams(vmem_limit_bytes=20 * 1024 * 1024),
        cost_estimate=pl.CostEstimate(flops=16 * rows * positions * (width + latent),
                                      bytes_accessed=positions * width * 2 + rows * (width + latent) * 2,
                                      transcendentals=rows * positions),
    )(scal, *args)


def merge(parts, latent, axis):
    lse = jnp.sum(parts[..., latent:latent + 3].astype(jnp.float32), axis=-1, keepdims=True)
    top = jnp.max(lse, axis=axis, keepdims=True)
    w = jnp.exp(lse - top)
    norm = jnp.sum(w, axis=axis)
    rows = jnp.sum(parts[..., :latent].astype(jnp.float32) * w, axis=axis) / norm
    return rows, jnp.squeeze(top, axis) + jnp.log(norm)


def merge_kernel(parts_ref, o_ref):
    slots, rows, width = o_ref.shape
    latent = width - LANES
    count = parts_ref.shape[0] // slots
    lane = lax.broadcasted_iota(jnp.int32, (rows, LANES), 1)
    for s in range(slots):
        parts = [parts_ref[s * count + i] for i in range(count)]
        lse = [jnp.sum(jnp.where(lane < 3, p[:, latent:].astype(jnp.float32), 0.0), axis=1, keepdims=True) for p in parts]
        top = functools.reduce(jnp.maximum, lse)
        w = [jnp.exp(v - top) for v in lse]
        norm = functools.reduce(jnp.add, w)
        total = functools.reduce(jnp.add, [p[:, :latent].astype(jnp.float32) * v for p, v in zip(parts, w)])
        o_ref[s, :, :latent] = (total / norm).astype(jnp.bfloat16)
        o_ref[s, :, latent:] = pack_columns(top + jnp.log(norm), lane)


def merge_slots(parts, slots):
    vm = pl.BlockSpec(memory_space=pltpu.VMEM)
    return pl.pallas_call(
        merge_kernel,
        in_specs=[vm],
        out_specs=vm,
        out_shape=jax.ShapeDtypeStruct((slots, *parts.shape[1:]), parts.dtype),
        compiler_params=pltpu.CompilerParams(vmem_limit_bytes=8 * 1024 * 1024),
        cost_estimate=pl.CostEstimate(flops=4 * parts.size, bytes_accessed=2 * parts.size, transcendentals=1024),
    )(parts)


def after(v, dep):
    return lax.optimization_barrier((v, dep))[0]


def second(parts, move):
    parts = regroup(parts)
    far = [move(parts[i], i) for i in range(4)]
    near = [move(after(parts[4 + i], far[i]), i) for i in range(4)]
    return far, near


def shards(cache, lengths, request_decode_slot, q_nope, q_rope, new_latent, w_key, value_up_weight):
    heads_dev, nope_dim, latent = w_key.shape
    req_dev, steps = q_nope.shape[:2]
    rope_dim = q_rope.shape[2] // heads_dev
    scale = (nope_dim + rope_dim) ** -0.5
    role, ctx, req = lax.axis_index("role"), lax.axis_index("ctx"), lax.axis_index("req")
    x, z = req // NZ, req % NZ
    ids = jnp.arange(request_decode_slot.shape[0], dtype=jnp.int32)
    blocks = jnp.swapaxes(cache, 1, 2)

    def move(c):
        return jnp.where(c == 1, 1, jnp.where(c == 2, -1, jnp.where(c == 3, 2 - 4 * (z % 2), 0)))

    outer, inner, far = ids // 8, ids % 4, 4 - ids // 4 % 2 * 4
    z_first = outer < NC
    dx, cls = jnp.where(z_first, inner, outer - NC), jnp.where(z_first, outer, inner)
    owner = (x + dx) % NX * NZ + (z + move(cls) + far + NZ) % NZ
    picked = pick(blocks, lookup(request_decode_slot, ids, 2 * owner + jnp.where(z_first, 1 - role, role)))
    queries = q_nope.reshape(req_dev, steps, heads_dev, nope_dim)
    absorbed = jnp.einsum("bshd,hdk->bshk", queries, w_key, preferred_element_type=jnp.float32).astype(jnp.bfloat16)
    own = jnp.concatenate([absorbed, q_rope.reshape(req_dev, steps, heads_dev, rope_dim)], axis=3)

    picked, both = lax.optimization_barrier((picked, (own, move_far(own))))
    both = jnp.stack(both, axis=1)
    heads = 2 * lax.axis_size("ctx")
    spread = jnp.broadcast_to(both[:, None], (req_dev, lax.axis_size("ctx"), *both.shape[1:]))
    every = lax.all_to_all(spread.reshape(heads, *both.shape[1:]), ("role", "ctx"), 0, 0, tiled=True)
    first = [move_z(picked[3], 3, 1), move_x(picked[6], 2), move_z(picked[1], 1, 1), move_x(picked[5], 1),
             move_z(picked[2], 2, 1), move_x(picked[7], 3), move_z(picked[0], 0, 1)]
    first, every = lax.optimization_barrier((first, every))
    got_z = [first[6], first[2], first[4], first[0]]
    got_x = [picked[4], first[3], first[1], first[5]]
    every = jnp.moveaxis(every, 1, 0).reshape(2, -1, latent + rope_dim)
    mine_f, mine_n = second(got_x, move_z)
    recv_f, recv_n = second(got_z, move_x)
    step = jnp.arange(NX * NC, dtype=jnp.int32)
    source = (x - step // NC + NX) % NX * NZ + (z - move(step % NC) + NZ) % NZ
    base = (ctx * (NX * NZ) + source) * LANES

    def scalars(far):
        length = lookup(request_decode_slot, lengths, 2 * (x * NZ + (z + far) % NZ) + role)
        return jnp.concatenate([length - base, role[None], ctx[None]]).astype(jnp.int32)

    part_f = attend(scalars(4), every[1], mine_f, recv_f, None, latent, scale)
    part_f = lax.all_to_all(part_f.reshape(heads, -1, latent + LANES), ("role", "ctx"), 0, 0, tiled=True)
    merged_f = merge_slots(part_f, req_dev)
    packed = move_far(merged_f)

    new = jnp.where(role == 0, new_latent[0], new_latent[1])
    new = jnp.pad(new, ((0, LANES - steps), (0, 0)))
    part_n = attend(scalars(0), every[0], mine_n, recv_n, new, latent, scale)
    part_n = after(part_n, merged_f)
    part_n = lax.all_to_all(part_n.reshape(heads, -1, latent + LANES), ("role", "ctx"), 0, 0, tiled=True)
    parts = jnp.concatenate([part_n.reshape(2, -1, *part_n.shape[1:]), packed[:, None]], axis=1)
    merged, _ = merge(parts, latent, 1)
    merged = merged.astype(jnp.bfloat16).reshape(req_dev, steps, heads_dev, latent)
    out = jnp.einsum("bshk,hkv->bshv", merged, value_up_weight, preferred_element_type=jnp.float32).astype(jnp.bfloat16)
    return out.reshape(req_dev, steps, -1)


def solution(mesh):
    placed = (
        P(None, ("ctx", "req"), "role"),
        P(),
        P(),
        P("req", None, ("role", "ctx")),
        P("req", None, ("role", "ctx")),
        P("req", None, None),
        P(("role", "ctx"), None, None),
        P(("role", "ctx"), None, None),
    )
    return jax.shard_map(
        shards,
        mesh=mesh,
        in_specs=placed,
        out_specs=P("req", None, ("role", "ctx")),
        check_vma=False,
    )
```
